512 devices in a mesh: shot: 64 (over x, z_lo, y), box: 8 (over z_hi, core).
Axes of the slice: x: 4, y: 8, z: 8 (z_hi: 4, z_lo: 2; z = z_hi * 2 + z_lo), core: 2. Of those that a mesh axis runs over, the one named last changes fastest.
Arguments:
- wave_prev: float32 [64, 64, 128, 128], P('shot', None, 'box'), may hold values from -6 to 6
- wave_now: float32 [64, 64, 128, 128], P('shot', None, 'box'), may hold values from -6 to 6
- adjoint_prev: float32 [64, 64, 128, 128], P('shot', None, 'box'), may hold values from -6 to 6
- adjoint_now: float32 [64, 64, 128, 128], P('shot', None, 'box'), may hold values from -6 to 6
- velocity: float32 [64, 128, 128], P(None, 'box'), may hold values from 0.2 to 0.42
- source_cell: int32 [64], P('shot'), may hold values from 0 to 1048575
- wavelet: float32 [64, 5], P('shot'), may hold values from -40 to 40
- receiver_cell: int32 [64, 128], P('shot'), may hold values from 2 to 1048450, as said below
- residual: float32 [64, 3, 128], P('shot'), may hold values from -40 to 40
Outputs:
- wave_out: float32 [64, 64, 128, 128], P('shot', None, 'box')
- adjoint_out: float32 [64, 64, 128, 128], P('shot', None, 'box')
- speed_out: float32 [64, 128, 128], P(None, 'box')
The draws below stay inside these ranges and needn't reach their ends.
Inputs may be any that keep to these rules, and one draw needn't show every extreme that they name: `receiver_cell`: each shot's 128 receiver cells are distinct and lie in the plane at depth 2; an index is (x * 128 + y) * 128 + z.
All inputs are finite; a program needn't handle non-finite values.
Results may differ from the reference program's by a relative error of at most 0.00002.
Values sent between devices are 32-bit elements; how exact they have to be, the bound alone decides.
A program may use at most 64 MiB of HBM per device.

```python
import jax
import jax.numpy as jnp
from jax import lax

NZ = 128
STEPS = 3
FINAL = 2
PASSES = 4
RECV = 128
RDEPTH = 2
SHOTS = 64
NX = 64
NY = 128


def draw_receiver_cell(key, part):
    shot_keys = jax.random.split(jax.random.fold_in(key, 7177), SHOTS)
    chosen = jax.vmap(lambda one_key: jax.random.permutation(one_key, NX * NY)[:RECV])(shot_keys)
    ends = jnp.array([0, NX * NY - 1], jnp.int32)
    chosen = chosen.astype(jnp.int32)
    first_row = chosen[0]
    has_low = jnp.any(first_row == 0)
    first_row = jnp.where(has_low, first_row, first_row.at[0].set(jnp.where(first_row[1] == 0, first_row[0], 0)))
    first_row = jnp.where(has_low, first_row, jnp.where(jnp.any(first_row == 0), first_row, first_row.at[1].set(0)))
    has_high = jnp.any(first_row == NX * NY - 1)
    position_high = jnp.where(first_row[RECV - 1] == 0, RECV - 2, RECV - 1)
    first_row = jnp.where(has_high, first_row, first_row.at[position_high].set(ends[1]))
    chosen = chosen.at[0].set(first_row)
    return (chosen * NZ + RDEPTH).astype(jnp.int32)


def touch_ends(values, stream_key, low, largest):
    shape = values.shape
    place = [jax.random.randint(jax.random.fold_in(stream_key, axis), (), 0, shape[axis]) for axis in range(len(shape))]
    values = values.at[tuple(place)].set(low)
    longest = shape.index(max(shape))
    place[longest] = (place[longest] + 1) % shape[longest]
    return values.at[tuple(place)].set(largest)


def levels(stream_key, dims, cuts, low, top_value):
    def one(dim, shards_of):
        steps = jax.random.uniform(jax.random.fold_in(jax.random.fold_in(stream_key, 6), dim), (shards_of,), jnp.float32, low / len(cuts), top_value / len(cuts))
        return jnp.repeat(jnp.exp(steps), dims[dim] // shards_of).reshape((-1,) + (1,) * (len(dims) - dim - 1))

    level = one(*cuts[0])
    for cut in cuts[1:]:
        level = level * one(*cut)
    return level


def gaussian(stream_key, dims, scale, limit, pieces=(), held_as=jnp.bfloat16):
    entries = scale * jax.random.normal(stream_key, dims, jnp.float32)
    if pieces:
        entries = entries * levels(stream_key, dims, pieces, -0.22, 0.18)
    return jnp.clip(entries, -limit, limit).astype(held_as)


def setup_inputs(seed: int = 0) -> dict:
    splits = jax.random.split(jax.random.key(seed), 10)
    return {
        "wave_prev": gaussian(splits[0], (SHOTS, NX, NY, NZ), 1.0, 6.0, ((0, 64), (2, 8)), jnp.float32),
        "wave_now": gaussian(splits[1], (SHOTS, NX, NY, NZ), 1.0, 6.0, ((0, 64), (2, 8)), jnp.float32),
        "adjoint_prev": gaussian(splits[2], (SHOTS, NX, NY, NZ), 1.0, 6.0, ((0, 64), (2, 8)), jnp.float32),
        "adjoint_now": gaussian(splits[3], (SHOTS, NX, NY, NZ), 1.0, 6.0, ((0, 64), (2, 8)), jnp.float32),
        "velocity": jnp.clip(0.2 + 0.21999998 * jax.random.uniform(splits[4], (NX, NY, NZ), jnp.float32) ** levels(splits[4], (NX, NY, NZ), ((1, 8),), -0.2, 0.2), 0.2, 0.42),
        "source_cell": touch_ends(jax.random.randint(splits[5], (SHOTS,), 0, NX * NY * NZ), jax.random.fold_in(splits[5], 1), 0, (NX * NY * NZ) - 1).astype(jnp.int32),
        "wavelet": gaussian(splits[6], (SHOTS, STEPS + FINAL), 8.0, 40.0, ((0, 64),), jnp.float32),
        "receiver_cell": draw_receiver_cell(jax.random.fold_in(splits[9], 71), 0),
        "residual": gaussian(splits[8], (SHOTS, STEPS, RECV), 8.0, 40.0, ((0, 64),), jnp.float32),
    }


stencil_weights = (-205.0 / 72.0, 8.0 / 5.0, -1.0 / 5.0, 8.0 / 315.0, -1.0 / 560.0)
conduct_scale = 1.0
diffuse_rate = 0.1
step_length = 0.1
speed_floor = 0.16
speed_ceiling = 0.44

def laplace(padded):
    count_first = padded.shape[-3] - 8
    count_second = padded.shape[-2] - 8
    count_third = padded.shape[-1] - 8

    def window(shift_first, shift_second, shift_third):
        return padded[..., 4 + shift_first:4 + shift_first + count_first, 4 + shift_second:4 + shift_second + count_second, 4 + shift_third:4 + shift_third + count_third]
    summed = 3.0 * stencil_weights[0] * window(0, 0, 0)
    for offset in range(1, 5):
        weight = stencil_weights[offset]
        summed = summed + weight * (window(offset, 0, 0) + window(-offset, 0, 0))
        summed = summed + weight * (window(0, offset, 0) + window(0, -offset, 0))
        summed = summed + weight * (window(0, 0, offset) + window(0, 0, -offset))
    return summed

def advance(earlier, current, speed_square):
    return 2.0 * current - earlier + speed_square * laplace(jnp.pad(current, 4))

def inject(wavefield, cell_index, values):
    flattened = wavefield.reshape(-1).at[cell_index].add(values)
    return flattened.reshape(wavefield.shape)

def conduct(rise):
    return rise / (1.0 + (rise / conduct_scale) ** 2)

def diffuse(smooth_in, padded, start_first, total_first, start_second, total_second):
    count_first = smooth_in.shape[0]
    count_second = smooth_in.shape[1]
    rise_first = padded[1:, 1:-1, :] - padded[:-1, 1:-1, :]
    face_first = start_first - 1 + lax.broadcasted_iota(jnp.int32, (count_first + 1, 1, 1), 0)
    interior_first = (face_first >= 0) & (face_first + 1 < total_first)
    flux_first = jnp.where(interior_first, conduct(rise_first), 0.0)
    rise_second = padded[1:-1, 1:, :] - padded[1:-1, :-1, :]
    face_second = start_second - 1 + lax.broadcasted_iota(jnp.int32, (1, count_second + 1, 1), 1)
    interior_second = (face_second >= 0) & (face_second + 1 < total_second)
    flux_second = jnp.where(interior_second, conduct(rise_second), 0.0)
    flux_third = conduct(smooth_in[:, :, 1:] - smooth_in[:, :, :-1])
    zero_face = jnp.zeros((count_first, count_second, 1), jnp.float32)
    flux_third = jnp.concatenate([zero_face, flux_third, zero_face], 2)
    change = flux_first[1:] - flux_first[:-1] + (flux_second[:, 1:] - flux_second[:, :-1]) + (flux_third[:, :, 1:] - flux_third[:, :, :-1])
    return smooth_in + diffuse_rate * change

def reference(wave_prev, wave_now, adjoint_prev, adjoint_now, velocity, source_cell, wavelet, receiver_cell, residual):
    speed_square = velocity * velocity
    blank = jnp.zeros(velocity.shape, jnp.float32)

    def one_shot(totals, items):
        earlier, current, adjoint_early, adjoint_current, source, amplitudes, receivers, residuals = items
        gradient_shot = blank
        illumination_shot = blank
        for step_index in range(STEPS):
            following = inject(advance(earlier, current, speed_square), source, amplitudes[step_index])
            adjoint_next = inject(advance(adjoint_early, adjoint_current, speed_square), receivers, residuals[step_index])
            second_diff = following - 2.0 * current + earlier
            gradient_shot = gradient_shot + adjoint_current * second_diff
            illumination_shot = illumination_shot + current * current
            earlier, current = (current, following)
            adjoint_early, adjoint_current = (adjoint_current, adjoint_next)
        return ((totals[0] + gradient_shot, totals[1] + illumination_shot), (earlier, current, adjoint_current))
    (gradient, illumination), (earliers, currents, adjoint_out) = lax.scan(one_shot, (blank, blank), (wave_prev, wave_now, adjoint_prev, adjoint_now, source_cell, wavelet, receiver_cell, residual))
    smoothed = gradient / jnp.sqrt(illumination + 1.0)
    for smooth_pass in range(PASSES):
        padded = jnp.pad(smoothed, ((1, 1), (1, 1), (0, 0)))
        smoothed = diffuse(smoothed, padded, 0, NX, 0, NY)
    speed_out = jnp.clip(velocity - step_length * smoothed, speed_floor, speed_ceiling)
    new_square = speed_out * speed_out

    def final_shot(items):
        earlier, current, source, amplitudes = items
        for step_index in range(FINAL):
            following = inject(advance(earlier, current, new_square), source, amplitudes[STEPS + step_index])
            earlier, current = (current, following)
        return current
    wave_out = lax.map(final_shot, (earliers, currents, source_cell, wavelet))
    return (wave_out, adjoint_out, speed_out)
```

```python
import functools

import jax
import jax.numpy as jnp
from jax import lax
from jax.experimental import pallas as pl
from jax.experimental.pallas import tpu as pltpu
from jax.sharding import PartitionSpec as P

MESH = pl.DeviceIdType.MESH
STEPS = 3
FINAL = 2
PASSES = 4
RDEPTH = 2
LANES = 128
H = 4
PAD = 8

stencil_weights = (-205.0 / 72.0, 8.0 / 5.0, -1.0 / 5.0, 8.0 / 315.0, -1.0 / 560.0)
diffuse_rate = 0.1
step_length = 0.1
speed_floor = 0.16
speed_ceiling = 0.44


def kernel(
    sizes,
    source_cell,
    wavelet,
    receiver_cell,
    residual,
    wave_prev,
    wave_now,
    adjoint_prev,
    adjoint_now,
    velocity,
    wave_out,
    adjoint_out,
    speed_out,
    staged,
    U,
    W,
    speed,
    square,
    received,
    G,
    I,
    rx,
    rz,
    ry,
    sx,
    sz,
    F,
    FA,
    FB,
    L,
    outs,
    in_sem,
    out_sem,
    halo_send,
    halo_recv,
    rs_send,
    rs_recv,
    ag_send,
    ag_recv,
):
    X, Z, Y, boxes, NX, R = sizes
    NY = R * boxes
    q, h, c = R // X, R // (X * Z), NX // Y
    shot, box = lax.axis_index("shot"), lax.axis_index("box")
    x = lax.div(shot, Z * Y)
    z = lax.rem(lax.div(shot, Y), Z)
    y = lax.rem(shot, Y)
    lower, upper = lax.max(box - 1, 0), lax.min(box + 1, boxes - 1)
    has_lower, has_upper = box > 0, box < boxes - 1

    def peer_x(d):
        return (lax.rem(x + d, X) * Z + z) * Y + y

    def peer_z(d):
        return (x * Z + lax.rem(z + d, Z)) * Y + y

    def peer_y(d):
        return (x * Z + z) * Y + lax.rem(y + d, Y)

    loads = [
        pltpu.make_async_copy(ref, staged.at[i], in_sem.at[i])
        for i, ref in enumerate((wave_now, adjoint_now, wave_prev, adjoint_prev, velocity))
    ]
    for load in loads:
        load.start()

    barrier = pltpu.get_barrier_semaphore()
    peers = (
        [peer_x(d) for d in range(1, X)]
        + [peer_z(d) for d in range(1, Z)]
        + [peer_y(d) for d in range(1, Y)]
    )
    for peer in peers:
        pl.semaphore_signal(barrier, inc=1, device_id={"shot": peer}, device_id_type=MESH)

    @pl.when(has_lower)
    def _():
        pl.semaphore_signal(barrier, inc=1, device_id={"box": lower}, device_id_type=MESH)

    @pl.when(has_upper)
    def _():
        pl.semaphore_signal(barrier, inc=1, device_id={"box": upper}, device_id_type=MESH)

    pad = jnp.zeros((R, PAD, LANES), jnp.float32)
    edge = jnp.zeros((H, NX, LANES), jnp.float32)
    for fields, slots in ((U, range(1, 6)), (W, range(1, 4))):
        for slot in slots:
            fields[slot, H : H + R, :PAD, :] = pad
            fields[slot, H : H + R, PAD + NX :, :] = pad

    @pl.when(box == 0)
    def _():
        for fields, slots in ((U, range(1, 6)), (W, range(1, 4))):
            for slot in slots:
                fields[slot, :H, PAD : PAD + NX, :] = edge
        F[:H] = edge

    @pl.when(box == boxes - 1)
    def _():
        for fields, slots in ((U, range(1, 6)), (W, range(1, 4))):
            for slot in slots:
                fields[slot, H + R :, PAD : PAD + NX, :] = edge
        F[H + R :] = edge

    class Halo:
        def __init__(self, ref, index, padded=True):
            def rows(start):
                if padded:
                    return ref.at[pl.ds(start, H), pl.ds(PAD, NX), :]
                return ref.at[pl.ds(start, H)]

            self.down = pltpu.make_async_remote_copy(
                src_ref=rows(H),
                dst_ref=rows(H + R),
                send_sem=halo_send.at[index, 0],
                recv_sem=halo_recv.at[index, 0],
                device_id={"box": lower},
                device_id_type=MESH,
            )
            self.up = pltpu.make_async_remote_copy(
                src_ref=rows(R),
                dst_ref=rows(0),
                send_sem=halo_send.at[index, 1],
                recv_sem=halo_recv.at[index, 1],
                device_id={"box": upper},
                device_id_type=MESH,
            )

        def start(self):
            pl.when(has_lower)(self.down.start)
            pl.when(has_upper)(self.up.start)

        def arrive(self):
            pl.when(has_lower)(self.up.wait_recv)
            pl.when(has_upper)(self.down.wait_recv)

        def leave(self):
            pl.when(has_lower)(self.down.wait_send)
            pl.when(has_upper)(self.up.wait_send)

    halo_u = {t: Halo(U.at[t], t - 1) for t in range(1, 6)}
    halo_w = {t: Halo(W.at[t], 4 + t) for t in range(1, 4)}
    halo_f = Halo(F, 8, padded=False)

    lane = lax.broadcasted_iota(jnp.int32, (1, LANES), 1)
    first = lax.broadcasted_iota(jnp.int32, (NX, 1), 0)
    flat = lax.broadcasted_iota(jnp.int32, (NX, LANES), 0) * (NY * LANES) + lax.broadcasted_iota(
        jnp.int32, (NX, LANES), 1
    )
    start_second = box * R
    source = source_cell[0]

    def over(begin, end, body):
        lax.fori_loop(begin, end, lambda r, carry: (body(r), carry)[1], 0)

    def over_edges(body):
        def step(i, carry):
            body(jnp.where(i < H, i, i + (R - 2 * H)))
            return carry

        lax.fori_loop(0, 2 * H, step, 0)

    def turned(i, r):
        return staged[i, pl.ds(r, NX, stride=R), :]

    def centre(r):
        return (H + r, pl.ds(PAD, NX), slice(None))

    def laplace(ref, r):
        field = ref[centre(r)]
        summed = (3.0 * stencil_weights[0]) * field
        for k in range(1, 5):
            weight = stencil_weights[k]
            around = (ref[H + r + k, pl.ds(PAD, NX), :] + ref[H + r - k, pl.ds(PAD, NX), :]) + (
                ref[H + r, pl.ds(PAD + k, NX), :] + ref[H + r, pl.ds(PAD - k, NX), :]
            )
            summed = summed + weight * around
            summed = summed + jnp.where(lane >= k, weight, 0.0) * pltpu.roll(field, k, 1)
            summed = summed + jnp.where(lane < LANES - k, weight, 0.0) * pltpu.roll(field, LANES - k, 1)
        return field, summed

    def injected(r, amplitude):
        return jnp.where(flat == source - (start_second + r) * LANES, amplitude, 0.0)

    pl.semaphore_wait(
        barrier, len(peers) + has_lower.astype(jnp.int32) + has_upper.astype(jnp.int32)
    )
    loads[0].wait()

    def turn_wave(r):
        U[(1, *centre(r))] = turned(0, r)

    over(0, R, turn_wave)
    halo_u[1].start()
    loads[1].wait()

    def turn_adjoint(r):
        W[(1, *centre(r))] = turned(1, r)

    over(0, R, turn_adjoint)
    halo_w[1].start()
    loads[2].wait()
    loads[3].wait()
    loads[4].wait()

    def turn_rest(r):
        U[(0, *centre(r))] = turned(2, r)
        W[(0, *centre(r))] = turned(3, r)
        v = turned(4, r)
        speed[r] = v
        square[r] = v * v
        here = (first * NY + (start_second + r)) * LANES + RDEPTH
        picks = jnp.where(receiver_cell[...] == here, 1.0, 0.0)
        for t in range(STEPS):
            sub = lax.broadcasted_iota(jnp.int32, (LANES, LANES), 0)
            values = jnp.where(sub == RDEPTH, residual[t : t + 1, :], 0.0)
            received[t, r] = lax.dot_general(
                picks,
                values,
                (((1,), (1,)), ((), ())),
                precision=lax.Precision.HIGHEST,
                preferred_element_type=jnp.float32,
            )

    over(0, R, turn_rest)

    def wave_row(t):
        now, early, later = U.at[t], U.at[t - 1], U.at[t + 1]
        amplitude = wavelet[0, t - 1]

        def body(r):
            field, summed = laplace(now, r)
            second_diff = square[r] * summed + injected(r, amplitude)
            later[centre(r)] = (2.0 * field - early[centre(r)]) + second_diff
            term = W[(t, *centre(r))] * second_diff
            G[r] = term if t == 1 else G[r] + term

        return body

    def adjoint_row(t, last=False):
        now, early = W.at[t], W.at[t - 1]

        def body(r):
            field, summed = laplace(now, r)
            value = (2.0 * field - early[centre(r)]) + (square[r] * summed + received[t - 1, r])
            if last:
                outs[1, pl.ds(r, NX, stride=R), :] = value
            else:
                W[(t + 1, *centre(r))] = value

        return body

    class Reduce:
        def __init__(self, which, ref):
            self.ref, self.which = ref, which
            self.x = []
            for d in range(1, X):
                target = lax.rem(x + d, X)
                self.x.append(self.copy(d - 1, ref.at[pl.ds(target * q, q)], rx.at[which, d - 1], peer_x(d)))
            self.z = []
            for d in range(1, Z):
                target = lax.rem(z + d, Z)
                self.z.append(
                    self.copy(X + d - 2, sx.at[which, pl.ds(target * h, h)], rz.at[which, d - 1], peer_z(d))
                )
            self.y = []
            for d in range(1, Y):
                target = lax.rem(y + d, Y)
                self.y.append(
                    self.copy(
                        X + Z + d - 3,
                        sz.at[which, :, pl.ds(pl.multiple_of(target * c, c), c), :],
                        ry.at[which, d - 1],
                        peer_y(d),
                    )
                )

        def copy(self, index, src, dst, peer):
            return pltpu.make_async_remote_copy(
                src_ref=src,
                dst_ref=dst,
                send_sem=rs_send.at[self.which, index],
                recv_sem=rs_recv.at[self.which, index],
                device_id={"shot": peer},
                device_id_type=MESH,
            )

        def start_x(self):
            for copy in self.x:
                copy.start()

        def then_z(self):
            for copy in self.x:
                copy.wait_recv()

            def add(r):
                total = self.ref[x * q + r]
                for d in range(1, X):
                    total = total + rx[self.which, d - 1, r]
                sx[self.which, r] = total

            over(0, q, add)
            for copy in self.z:
                copy.start()

        def then_y(self):
            for copy in self.z:
                copy.wait_recv()

            def add(r):
                total = sx[self.which, z * h + r]
                for d in range(1, Z):
                    total = total + rz[self.which, d - 1, r]
                sz[self.which, r] = total

            over(0, h, add)
            for copy in self.y:
                copy.start()

        def piece(self):
            for copy in self.y:
                copy.wait_recv()
            total = sz[self.which, :, pl.ds(pl.multiple_of(y * c, c), c), :]
            for d in range(1, Y):
                total = total + ry[self.which, d - 1]
            return total

        def leave(self):
            for copy in self.x + self.z + self.y:
                copy.wait_send()

    reduce_g, reduce_i = Reduce(0, G), Reduce(1, I)

    for t in range(1, STEPS):
        over(H, R - H, wave_row(t))
        halo_u[t].arrive()
        over_edges(wave_row(t))
        halo_u[t + 1].start()
        over(H, R - H, adjoint_row(t))
        halo_w[t].arrive()
        over_edges(adjoint_row(t))
        halo_w[t + 1].start()

    def light(r):
        one, two, three = (U[(t, *centre(r))] for t in range(1, 4))
        I[r] = (one * one + two * two) + three * three

    over(0, R, light)
    reduce_i.start_x()
    over(H, R - H, wave_row(STEPS))
    halo_u[STEPS].arrive()
    over_edges(wave_row(STEPS))
    halo_u[STEPS + 1].start()
    reduce_g.start_x()
    reduce_i.then_z()
    over(H, R - H, adjoint_row(STEPS, last=True))
    halo_w[STEPS].arrive()
    over_edges(adjoint_row(STEPS, last=True))
    adjoint_store = pltpu.make_async_copy(outs.at[1], adjoint_out, out_sem.at[1])
    adjoint_store.start()
    reduce_i.then_y()

    reduce_g.then_z()

    def last_laplace(r):
        L[r] = laplace(U.at[STEPS + 1], r)[1]

    over(H, R - H, last_laplace)
    reduce_g.then_y()
    halo_u[STEPS + 1].arrive()
    over_edges(last_laplace)
    illumination = reduce_i.piece()
    gradient = reduce_g.piece()

    row = H + x * q + z * h
    F[pl.ds(row, h), pl.ds(pl.multiple_of(y * c, c), c), :] = gradient / jnp.sqrt(illumination + 1.0)

    def share(index, part, peer):
        return pltpu.make_async_remote_copy(
            src_ref=part,
            dst_ref=part,
            send_sem=ag_send.at[index],
            recv_sem=ag_recv.at[index],
            device_id={"shot": peer},
            device_id_type=MESH,
        )

    part_y = F.at[pl.ds(row, h), pl.ds(pl.multiple_of(y * c, c), c), :]
    shares = [share(X + Z + d - 3, part_y, peer_y(d)) for d in range(1, Y)]
    for copy in shares:
        copy.start()
    for copy in shares:
        copy.wait_recv()
    sent = shares
    part_z = F.at[pl.ds(row, h)]
    shares = [share(X + d - 2, part_z, peer_z(d)) for d in range(1, Z)]
    for copy in shares:
        copy.start()
    for copy in shares:
        copy.wait_recv()
    sent = sent + shares
    part_x = F.at[pl.ds(H + x * q, q)]
    shares = [share(d - 1, part_x, peer_x(d)) for d in range(1, X)]
    for copy in shares:
        copy.start()
    for copy in shares:
        copy.wait_recv()
    sent = sent + shares
    halo_f.start()
    halo_f.arrive()

    def conduct(rise):
        return rise / (1.0 + rise * rise)

    def diffuse(src, last, put):
        def face(r, rise):
            at = start_second + (r - H)
            return jnp.where((at > 0) & (at < NY), conduct(rise), 0.0)

        begin, end = last + 1, R + 2 * H - 1 - last

        def body(r, carry):
            below, field = carry
            higher = src[r + 1]
            above = face(r + 1, higher - field)
            along_first = jnp.where(first < NX - 1, conduct(pltpu.roll(field, NX - 1, 0) - field), 0.0)
            along_third = jnp.where(lane < LANES - 1, conduct(pltpu.roll(field, LANES - 1, 1) - field), 0.0)
            change = (
                (along_first - pltpu.roll(along_first, 1, 0))
                + (above - below)
                + (along_third - pltpu.roll(along_third, 1, 1))
            )
            put(r, field + diffuse_rate * change)
            return above, higher

        field = src[begin]
        lax.fori_loop(begin, end, body, (face(begin, field - src[begin - 1]), field))

    def into(ref):
        def put(r, value):
            ref[r] = value

        return put

    def update(r, value):
        new_speed = jnp.clip(speed[r - H] - step_length * value, speed_floor, speed_ceiling)
        outs[2, pl.ds(r - H, NX, stride=R), :] = new_speed
        square[r - H] = new_speed * new_speed

    diffuse(F, 0, into(FA))
    diffuse(FA, 1, into(FB))
    diffuse(FB, 2, into(FA))
    diffuse(FA, 3, update)
    speed_store = pltpu.make_async_copy(outs.at[2], speed_out, out_sem.at[2])
    speed_store.start()

    def final_one(r):
        value = (2.0 * U[(STEPS + 1, *centre(r))] - U[(STEPS, *centre(r))]) + (
            square[r] * L[r] + injected(r, wavelet[0, STEPS])
        )
        U[(STEPS + 2, *centre(r))] = value

    def final_two(r):
        field, summed = laplace(U.at[STEPS + 2], r)
        outs[0, pl.ds(r, NX, stride=R), :] = (2.0 * field - U[(STEPS + 1, *centre(r))]) + (
            square[r] * summed + injected(r, wavelet[0, STEPS + 1])
        )

    over_edges(final_one)
    halo_u[STEPS + 2].start()
    over(H, R - H, final_one)
    over(H, R - H, final_two)
    halo_u[STEPS + 2].arrive()
    over_edges(final_two)
    wave_store = pltpu.make_async_copy(outs.at[0], wave_out, out_sem.at[0])
    wave_store.start()

    for halo in (*halo_u.values(), *halo_w.values(), halo_f):
        halo.leave()
    reduce_g.leave()
    reduce_i.leave()
    for copy in sent:
        copy.wait_send()
    adjoint_store.wait()
    speed_store.wait()
    wave_store.wait()


def local(
    parts,
    boxes,
    wave_prev,
    wave_now,
    adjoint_prev,
    adjoint_now,
    velocity,
    source_cell,
    wavelet,
    receiver_cell,
    residual,
):
    X, Z, Y = parts
    NX, R, D = velocity.shape
    q, h, c = R // X, R // (X * Z), NX // Y
    f32 = jnp.float32
    flat = (NX * R, D)
    padded = (R + 2 * H, NX + 2 * PAD, D)
    plain = (R, NX, D)
    around = (R + 2 * H, NX, D)
    n_rs = X + Y + Z - 3
    vmem, smem, anywhere = (
        pl.BlockSpec(memory_space=pltpu.VMEM),
        pl.BlockSpec(memory_space=pltpu.SMEM),
        pl.BlockSpec(memory_space=pl.ANY),
    )
    out = jax.ShapeDtypeStruct(flat, f32)
    wave_out, adjoint_out, speed_out = pl.pallas_call(
        functools.partial(kernel, (X, Z, Y, boxes, NX, R)),
        out_shape=(out, out, out),
        in_specs=[smem, smem, vmem, vmem] + [anywhere] * 5,
        out_specs=(anywhere, anywhere, anywhere),
        scratch_shapes=[
            pltpu.VMEM((5, *flat), f32),
            pltpu.VMEM((6, *padded), f32),
            pltpu.VMEM((4, *padded), f32),
            pltpu.VMEM(plain, f32),
            pltpu.VMEM(plain, f32),
            pltpu.VMEM((STEPS, *plain), f32),
            pltpu.VMEM(plain, f32),
            pltpu.VMEM(plain, f32),
            pltpu.VMEM((2, max(X - 1, 1), q, NX, D), f32),
            pltpu.VMEM((2, max(Z - 1, 1), h, NX, D), f32),
            pltpu.VMEM((2, max(Y - 1, 1), h, c, D), f32),
            pltpu.VMEM((2, q, NX, D), f32),
            pltpu.VMEM((2, h, NX, D), f32),
            pltpu.VMEM(around, f32),
            pltpu.VMEM(around, f32),
            pltpu.VMEM(around, f32),
            pltpu.VMEM(plain, f32),
            pltpu.VMEM((3, *flat), f32),
            pltpu.SemaphoreType.DMA((5,)),
            pltpu.SemaphoreType.DMA((3,)),
            pltpu.SemaphoreType.DMA((9, 2)),
            pltpu.SemaphoreType.DMA((9, 2)),
            pltpu.SemaphoreType.DMA((2, n_rs)),
            pltpu.SemaphoreType.DMA((2, n_rs)),
            pltpu.SemaphoreType.DMA((n_rs,)),
            pltpu.SemaphoreType.DMA((n_rs,)),
        ],
        compiler_params=pltpu.CompilerParams(
            collective_id=0, has_side_effects=True, vmem_limit_bytes=56 * 1024 * 1024
        ),
    )(
        source_cell,
        wavelet,
        receiver_cell,
        residual.reshape(residual.shape[1:]),
        wave_prev.reshape(flat),
        wave_now.reshape(flat),
        adjoint_prev.reshape(flat),
        adjoint_now.reshape(flat),
        velocity.reshape(flat),
    )
    field = (1, NX, R, D)
    return wave_out.reshape(field), adjoint_out.reshape(field), speed_out.reshape(field[1:])


def solution(mesh):
    shots, boxes = mesh.shape["shot"], mesh.shape["box"]
    parts = {64: (4, 2, 8), 16: (4, 2, 2), 8: (4, 2, 1)}[shots]
    return jax.shard_map(
        functools.partial(local, parts, boxes),
        mesh=mesh,
        in_specs=(
            P("shot", None, "box", None),
            P("shot", None, "box", None),
            P("shot", None, "box", None),
            P("shot", None, "box", None),
            P(None, "box", None),
            P("shot"),
            P("shot", None),
            P("shot", None),
            P("shot", None, None),
        ),
        out_specs=(
            P("shot", None, "box", None),
            P("shot", None, "box", None),
            P(None, "box", None),
        ),
        check_vma=False,
    )
```

```python
import functools

import jax
import jax.numpy as jnp
from jax import lax
from jax.experimental import pallas as pl
from jax.experimental.pallas import tpu as pltpu
from jax.sharding import PartitionSpec as P

MESH = pl.DeviceIdType.MESH
STEPS = 3
FINAL = 2
PASSES = 4
RDEPTH = 2
LANES = 128
H = 4
PAD = 8

stencil_weights = (-205.0 / 72.0, 8.0 / 5.0, -1.0 / 5.0, 8.0 / 315.0, -1.0 / 560.0)
diffuse_rate = 0.1
step_length = 0.1
speed_floor = 0.16
speed_ceiling = 0.44


def kernel(
    sizes,
    source_cell,
    wavelet,
    receiver_cell,
    residual,
    wave_prev,
    wave_now,
    adjoint_prev,
    adjoint_now,
    velocity,
    wave_out,
    adjoint_out,
    speed_out,
    staged,
    U,
    W,
    speed,
    square,
    received,
    G,
    I,
    rx,
    rz,
    ry,
    sx,
    sz,
    E,
    S,
    L,
    zu,
    zw,
    outs,
    in_sem,
    out_sem,
    halo_send,
    halo_recv,
    rs_send,
    rs_recv,
    ag_send,
    ag_recv,
    near_send,
    near_recv,
):
    X, Z, Y, boxes, NX, R = sizes
    NY = R * boxes
    q, h, c = R // X, R // (X * Z), NX // Y
    shot, box = lax.axis_index("shot"), lax.axis_index("box")
    x = lax.div(shot, Z * Y)
    z = lax.rem(lax.div(shot, Y), Z)
    y = lax.rem(shot, Y)
    lower, upper = lax.max(box - 1, 0), lax.min(box + 1, boxes - 1)
    has_lower, has_upper = box > 0, box < boxes - 1

    def peer_x(d):
        return (lax.rem(x + d, X) * Z + z) * Y + y

    def peer_z(d):
        return (x * Z + lax.rem(z + d, Z)) * Y + y

    def peer_y(d):
        return (x * Z + z) * Y + lax.rem(y + d, Y)

    pieces = X * Z
    place = box * pieces + x * Z + z
    reach = -(-H // h)
    beside = [e for e in (-1, 0, 1) if Y > 1 or e == 0]
    near = [(d, e) for d in range(-reach, reach + 1) for e in beside if (d, e) != (0, 0)]

    def is_near(d, e):
        return (place + d >= 0) & (place + d < boxes * pieces) & (y + e >= 0) & (y + e < Y)

    def owner(d, e):
        other = lax.clamp(0, place + d, boxes * pieces - 1)
        return {
            "shot": lax.rem(other, pieces) * Y + lax.clamp(0, y + e, Y - 1),
            "box": lax.div(other, pieces),
        }

    E[...] = jnp.zeros_like(E)

    loads = [
        pltpu.make_async_copy(ref, staged.at[i], in_sem.at[i])
        for i, ref in enumerate((wave_now, adjoint_now, wave_prev, adjoint_prev, velocity))
    ]
    for load in loads:
        load.start()

    barrier = pltpu.get_barrier_semaphore()
    peers = (
        [peer_x(d) for d in range(1, X)]
        + [peer_z(d) for d in range(1, Z)]
        + [peer_y(d) for d in range(1, Y)]
    )
    for peer in peers:
        pl.semaphore_signal(barrier, inc=1, device_id={"shot": peer}, device_id_type=MESH)

    @pl.when(has_lower)
    def _():
        pl.semaphore_signal(barrier, inc=1, device_id={"box": lower}, device_id_type=MESH)

    @pl.when(has_upper)
    def _():
        pl.semaphore_signal(barrier, inc=1, device_id={"box": upper}, device_id_type=MESH)

    count = len(peers) + has_lower.astype(jnp.int32) + has_upper.astype(jnp.int32)
    for d, e in near:

        @pl.when(is_near(d, e))
        def _(d=d, e=e):
            pl.semaphore_signal(barrier, inc=1, device_id=owner(d, e), device_id_type=MESH)

        count = count + is_near(d, e).astype(jnp.int32)

    pad = jnp.zeros((R, PAD, LANES), jnp.float32)
    edge = jnp.zeros((H, NX, LANES), jnp.float32)
    for fields, slots in ((U, range(1, 6)), (W, range(1, 4))):
        for slot in slots:
            fields[slot, H : H + R, :PAD, :] = pad
            fields[slot, H : H + R, PAD + NX :, :] = pad

    @pl.when(box == 0)
    def _():
        for fields, slots in ((U, range(1, 6)), (W, range(1, 4))):
            for slot in slots:
                fields[slot, :H, PAD : PAD + NX, :] = edge

    @pl.when(box == boxes - 1)
    def _():
        for fields, slots in ((U, range(1, 6)), (W, range(1, 4))):
            for slot in slots:
                fields[slot, H + R :, PAD : PAD + NX, :] = edge

    class Halo:
        def __init__(self, ref, index):
            def rows(start):
                return ref.at[pl.ds(start, H), pl.ds(PAD, NX), :]

            self.down = pltpu.make_async_remote_copy(
                src_ref=rows(H),
                dst_ref=rows(H + R),
                send_sem=halo_send.at[index, 0],
                recv_sem=halo_recv.at[index, 0],
                device_id={"box": lower},
                device_id_type=MESH,
            )
            self.up = pltpu.make_async_remote_copy(
                src_ref=rows(R),
                dst_ref=rows(0),
                send_sem=halo_send.at[index, 1],
                recv_sem=halo_recv.at[index, 1],
                device_id={"box": upper},
                device_id_type=MESH,
            )

        def start(self):
            pl.when(has_lower)(self.down.start)
            pl.when(has_upper)(self.up.start)

        def arrive(self):
            pl.when(has_lower)(self.up.wait_recv)
            pl.when(has_upper)(self.down.wait_recv)

        def leave(self):
            pl.when(has_lower)(self.down.wait_send)
            pl.when(has_upper)(self.up.wait_send)

    halo_u = {t: Halo(U.at[t], t - 1) for t in range(1, 6)}
    halo_w = {t: Halo(W.at[t], 4 + t) for t in range(1, 4)}

    lane = lax.broadcasted_iota(jnp.int32, (1, LANES), 1)
    first = lax.broadcasted_iota(jnp.int32, (NX, 1), 0)
    flat = lax.broadcasted_iota(jnp.int32, (NX, LANES), 0) * (NY * LANES) + lax.broadcasted_iota(
        jnp.int32, (NX, LANES), 1
    )
    start_second = box * R
    source = source_cell[0]

    def over(begin, end, body):
        lax.fori_loop(begin, end, lambda r, carry: (body(r), carry)[1], 0)

    def over_edges(body):
        def step(i, carry):
            body(jnp.where(i < H, i, i + (R - 2 * H)))
            return carry

        lax.fori_loop(0, 2 * H, step, 0)

    def turned(i, r):
        return staged[i, pl.ds(r, NX, stride=R), :]

    def centre(r):
        return (H + r, pl.ds(PAD, NX), slice(None))

    apart = lax.broadcasted_iota(jnp.int32, (LANES, LANES), 0) - lax.broadcasted_iota(
        jnp.int32, (LANES, LANES), 1
    )
    along_depth = jnp.where(apart == 0, 3.0 * stencil_weights[0], 0.0)
    for k in range(1, 5):
        along_depth = along_depth + jnp.where((apart == k) | (apart == -k), stencil_weights[k], 0.0)

    def depth(ref, out):
        field = ref[pl.ds(H, R), pl.ds(PAD, NX), :].reshape(R * NX, LANES)
        out[...] = lax.dot_general(
            field,
            along_depth,
            (((1,), (0,)), ((), ())),
            precision=lax.Precision.HIGHEST,
            preferred_element_type=jnp.float32,
        ).reshape(R, NX, LANES)

    def laplace(ref, along, r):
        summed = along[r]
        for k in range(1, 5):
            around = (ref[H + r + k, pl.ds(PAD, NX), :] + ref[H + r - k, pl.ds(PAD, NX), :]) + (
                ref[H + r, pl.ds(PAD + k, NX), :] + ref[H + r, pl.ds(PAD - k, NX), :]
            )
            summed = summed + stencil_weights[k] * around
        return summed

    def injected(r, amplitude):
        return jnp.where(flat == source - (start_second + r) * LANES, amplitude, 0.0)

    def wave_row(t):
        now, early, later = U.at[t], U.at[t - 1], U.at[t + 1]
        amplitude = wavelet[0, t - 1]

        def body(r):
            field = now[centre(r)]
            second_diff = square[r] * laplace(now, zu, r) + injected(r, amplitude)
            later[centre(r)] = (2.0 * field - early[centre(r)]) + second_diff
            term = W[(t, *centre(r))] * second_diff
            G[r] = term if t == 1 else G[r] + term

        return body

    def adjoint_row(t, last=False):
        now, early = W.at[t], W.at[t - 1]

        def body(r):
            value = (2.0 * now[centre(r)] - early[centre(r)]) + (
                square[r] * laplace(now, zw, r) + received[t - 1, r]
            )
            if last:
                outs[1, pl.ds(r, NX, stride=R), :] = value
            else:
                W[(t + 1, *centre(r))] = value

        return body

    pl.semaphore_wait(barrier, count)
    loads[0].wait()

    def turn_wave(r):
        U[(1, *centre(r))] = turned(0, r)

    over(0, R, turn_wave)
    halo_u[1].start()
    loads[1].wait()

    def turn_adjoint(r):
        W[(1, *centre(r))] = turned(1, r)

    over(0, R, turn_adjoint)
    halo_w[1].start()
    depth(U.at[1], zu)
    loads[2].wait()
    loads[3].wait()
    loads[4].wait()

    def turn_rest(r):
        U[(0, *centre(r))] = turned(2, r)
        W[(0, *centre(r))] = turned(3, r)
        v = turned(4, r)
        speed[r] = v
        square[r] = v * v

    over(0, R, turn_rest)
    over(H, R - H, wave_row(1))

    def receive():
        shape = (R, NX, LANES)
        here = (
            lax.broadcasted_iota(jnp.int32, shape, 1) * NY
            + lax.broadcasted_iota(jnp.int32, shape, 0)
            + start_second
        ) * LANES + RDEPTH
        picks = jnp.where(here == receiver_cell[...].reshape(1, 1, LANES), 1.0, 0.0)
        picks = picks.astype(jnp.bfloat16).reshape(R * NX, LANES)
        at_depth = lax.broadcasted_iota(jnp.int32, (LANES, LANES), 0) == RDEPTH
        for t in range(STEPS):
            rest, total = jnp.where(at_depth, residual[t], 0.0), None
            for _ in range(3):
                part = rest.astype(jnp.bfloat16)
                rest = rest - part.astype(jnp.float32)
                picked = lax.dot_general(
                    picks, part, (((1,), (1,)), ((), ())), preferred_element_type=jnp.float32
                )
                total = picked if total is None else total + picked
            received[t] = total.reshape(shape)

    receive()
    depth(W.at[1], zw)

    class Reduce:
        def __init__(self, which, ref):
            self.ref, self.which = ref, which
            self.x = []
            for d in range(1, X):
                target = lax.rem(x + d, X)
                self.x.append(self.copy(d - 1, ref.at[pl.ds(target * q, q)], rx.at[which, d - 1], peer_x(d)))
            self.z = []
            for d in range(1, Z):
                target = lax.rem(z + d, Z)
                self.z.append(
                    self.copy(X + d - 2, sx.at[which, pl.ds(target * h, h)], rz.at[which, d - 1], peer_z(d))
                )
            self.y = []
            for d in range(1, Y):
                target = lax.rem(y + d, Y)
                self.y.append(
                    self.copy(
                        X + Z + d - 3,
                        sz.at[which, :, pl.ds(pl.multiple_of(target * c, c), c), :],
                        ry.at[which, d - 1],
                        peer_y(d),
                    )
                )

        def copy(self, index, src, dst, peer):
            return pltpu.make_async_remote_copy(
                src_ref=src,
                dst_ref=dst,
                send_sem=rs_send.at[self.which, index],
                recv_sem=rs_recv.at[self.which, index],
                device_id={"shot": peer},
                device_id_type=MESH,
            )

        def start_x(self, part):
            d = lax.rem(part - x + X, X)

            @pl.when(d > 0)
            def _():
                slot = lax.max(d - 1, 0)
                self.copy(
                    slot, self.ref.at[pl.ds(part * q, q)], rx.at[self.which, slot], peer_x(d)
                ).start()

        def then_z(self):
            for copy in self.x:
                copy.wait_recv()

            def add(r):
                total = self.ref[x * q + r]
                for d in range(1, X):
                    total = total + rx[self.which, d - 1, r]
                sx[self.which, r] = total

            over(0, q, add)
            for copy in self.z:
                copy.start()

        def then_y(self):
            for copy in self.z:
                copy.wait_recv()

            def add(r):
                total = sx[self.which, z * h + r]
                for d in range(1, Z):
                    total = total + rz[self.which, d - 1, r]
                sz[self.which, r] = total

            over(0, h, add)
            for copy in self.y:
                copy.start()

        def piece(self):
            for copy in self.y:
                copy.wait_recv()
            total = sz[self.which, :, pl.ds(pl.multiple_of(y * c, c), c), :]
            for d in range(1, Y):
                total = total + ry[self.which, d - 1]
            return total

        def leave(self):
            for copy in self.x + self.z + self.y:
                copy.wait_send()

    reduce_g, reduce_i = Reduce(0, G), Reduce(1, I)

    for t in range(1, STEPS):
        if t > 1:
            over(H, R - H, wave_row(t))
        halo_u[t].arrive()
        over_edges(wave_row(t))
        halo_u[t + 1].start()
        over(H, R - H, adjoint_row(t))
        halo_w[t].arrive()
        over_edges(adjoint_row(t))
        halo_w[t + 1].start()
        depth(U.at[t + 1], zu)
        if t + 1 < STEPS:
            depth(W.at[t + 1], zw)

    def light(r):
        one, two, three = (U[(t, *centre(r))] for t in range(1, 4))
        I[r] = (one * one + two * two) + three * three

    over(0, R, light)
    for part in range(X):
        reduce_i.start_x(part)
    over(H, R - H, wave_row(STEPS))
    for part in range(1, X - 1):
        reduce_g.start_x(part)
    halo_u[STEPS].arrive()
    over_edges(wave_row(STEPS))
    for part in (0, X - 1):
        reduce_g.start_x(part)
    halo_u[STEPS + 1].start()
    reduce_i.then_z()
    depth(W.at[STEPS], zw)
    over(H, R - H, adjoint_row(STEPS, last=True))
    halo_w[STEPS].arrive()
    over_edges(adjoint_row(STEPS, last=True))
    adjoint_store = pltpu.make_async_copy(outs.at[1], adjoint_out, out_sem.at[1])
    adjoint_store.start()
    reduce_i.then_y()

    depth(U.at[STEPS + 1], zu)

    def before_update(r):
        L[r] = laplace(U.at[STEPS + 1], zu, r)
        U[(STEPS + 2, *centre(r))] = (
            2.0 * U[(STEPS + 1, *centre(r))] - U[(STEPS, *centre(r))]
        ) + injected(r, wavelet[0, STEPS])

    over(H, R - H, before_update)
    halo_u[STEPS + 1].arrive()
    over_edges(before_update)
    illumination = reduce_i.piece()
    reduce_g.then_z()
    reduce_g.then_y()
    gradient = reduce_g.piece()

    E[pl.ds(H, h), pl.ds(c, c), :] = gradient / jnp.sqrt(illumination + 1.0)

    def index_of(d, e):
        return (d + reach) * 3 + e + 1

    def to_near(d, e):
        return pltpu.make_async_remote_copy(
            src_ref=E.at[pl.ds(H, h), pl.ds(c, c), :],
            dst_ref=E.at[pl.ds(H - d * h, h), pl.ds(c - e * c, c), :],
            send_sem=near_send.at[index_of(d, e)],
            recv_sem=near_recv.at[index_of(-d, -e)],
            device_id=owner(d, e),
            device_id_type=MESH,
        )

    for d, e in near:
        pl.when(is_near(d, e))(to_near(d, e).start)
    for d, e in near:
        pl.when(is_near(d, e))(to_near(-d, -e).wait_recv)

    row = x * q + z * h
    at_first = y * c - c + lax.broadcasted_iota(jnp.int32, (1, 3 * c, 1), 1)
    face_first = (at_first >= 0) & (at_first + 1 < NX)
    face_third = lax.broadcasted_iota(jnp.int32, (1, 1, LANES), 2) < LANES - 1

    def conduct(rise):
        return rise / (1.0 + rise * rise)

    smoothed = E[...]
    for turn in range(PASSES):
        rows = smoothed.shape[0]
        at_second = (start_second + row - H + turn + 1) + lax.broadcasted_iota(
            jnp.int32, (rows - 1, 1, 1), 0
        )
        face_second = (at_second > 0) & (at_second < NY)
        second = jnp.where(face_second, conduct(smoothed[1:] - smoothed[:-1]), 0.0)
        field = smoothed[1:-1]
        along_first = jnp.where(face_first, conduct(pltpu.roll(field, 3 * c - 1, 1) - field), 0.0)
        along_third = jnp.where(face_third, conduct(pltpu.roll(field, LANES - 1, 2) - field), 0.0)
        change = (
            (along_first - pltpu.roll(along_first, 1, 1))
            + (second[1:] - second[:-1])
            + (along_third - pltpu.roll(along_third, 1, 2))
        )
        smoothed = field + diffuse_rate * change
    mine = pl.ds(row, h), pl.ds(pl.multiple_of(y * c, c), c), slice(None)
    S[mine] = jnp.clip(speed[mine] - step_length * smoothed[:, c : 2 * c], speed_floor, speed_ceiling)

    def share(index, part, peer):
        return pltpu.make_async_remote_copy(
            src_ref=part,
            dst_ref=part,
            send_sem=ag_send.at[index],
            recv_sem=ag_recv.at[index],
            device_id={"shot": peer},
            device_id_type=MESH,
        )

    by_y = [share(X + Z + d - 3, S.at[mine], peer_y(d)) for d in range(1, Y)]
    for copy in by_y:
        copy.start()
    for copy in by_y:
        copy.wait_recv()
    by_z = [share(X + d - 2, S.at[pl.ds(row, h)], peer_z(d)) for d in range(1, Z)]
    for copy in by_z:
        copy.start()
    for copy in by_z:
        copy.wait_recv()
    by_x = [share(d - 1, S.at[pl.ds(x * q, q)], peer_x(d)) for d in range(1, X)]
    for copy in by_x:
        copy.start()

    def final_one(r):
        new_speed = S[r]
        outs[2, pl.ds(r, NX, stride=R), :] = new_speed
        new_square = new_speed * new_speed
        square[r] = new_square
        U[(STEPS + 2, *centre(r))] = U[(STEPS + 2, *centre(r))] + new_square * L[r]

    def final_two(r):
        outs[0, pl.ds(r, NX, stride=R), :] = (
            2.0 * U[(STEPS + 2, *centre(r))] - U[(STEPS + 1, *centre(r))]
        ) + (square[r] * laplace(U.at[STEPS + 2], zu, r) + injected(r, wavelet[0, STEPS + 1]))

    def part_of_first(part):
        d = lax.rem(x - part + X, X)

        @pl.when(d > 0)
        def _():
            share(lax.max(d - 1, 0), S.at[pl.ds(part * q, q)], peer_x(d)).wait_recv()

        over(part * q, part * q + q, final_one)

    for part in (0, X - 1):
        part_of_first(part)
    halo_u[STEPS + 2].start()
    for part in range(1, X - 1):
        part_of_first(part)
    speed_store = pltpu.make_async_copy(outs.at[2], speed_out, out_sem.at[2])
    speed_store.start()
    depth(U.at[STEPS + 2], zu)
    over(H, R - H, final_two)
    halo_u[STEPS + 2].arrive()
    over_edges(final_two)
    wave_store = pltpu.make_async_copy(outs.at[0], wave_out, out_sem.at[0])
    wave_store.start()

    for halo in (*halo_u.values(), *halo_w.values()):
        halo.leave()
    reduce_g.leave()
    reduce_i.leave()
    for d, e in near:
        pl.when(is_near(d, e))(to_near(d, e).wait_send)
    for copy in by_y + by_z + by_x:
        copy.wait_send()
    adjoint_store.wait()
    speed_store.wait()
    wave_store.wait()


def hand_over(wave, adjoint, speed, wave_out, adjoint_out, speed_out, sem):
    copies = [
        pltpu.make_async_copy(src, dst, sem.at[i])
        for i, (src, dst) in enumerate(((wave, wave_out), (adjoint, adjoint_out), (speed, speed_out)))
    ]
    for copy in copies:
        copy.start()
    for copy in copies:
        copy.wait()


def local(
    parts,
    boxes,
    wave_prev,
    wave_now,
    adjoint_prev,
    adjoint_now,
    velocity,
    source_cell,
    wavelet,
    receiver_cell,
    residual,
):
    X, Z, Y = parts
    NX, R, D = velocity.shape
    q, h, c = R // X, R // (X * Z), NX // Y
    f32 = jnp.float32
    flat = (NX * R, D)
    padded = (R + 2 * H, NX + 2 * PAD, D)
    plain = (R, NX, D)
    n_rs = X + Y + Z - 3
    n_near = 3 * (2 * -(-H // h) + 1)
    vmem, smem, anywhere = (
        pl.BlockSpec(memory_space=pltpu.VMEM),
        pl.BlockSpec(memory_space=pltpu.SMEM),
        pl.BlockSpec(memory_space=pl.ANY),
    )
    out = jax.ShapeDtypeStruct(flat, f32)
    wave_out, adjoint_out, speed_out = pl.pallas_call(
        functools.partial(kernel, (X, Z, Y, boxes, NX, R)),
        out_shape=(out, out, out),
        in_specs=[smem, smem, vmem, vmem] + [anywhere] * 5,
        out_specs=(anywhere, anywhere, anywhere),
        scratch_shapes=[
            pltpu.VMEM((5, *flat), f32),
            pltpu.VMEM((6, *padded), f32),
            pltpu.VMEM((4, *padded), f32),
            pltpu.VMEM(plain, f32),
            pltpu.VMEM(plain, f32),
            pltpu.VMEM((STEPS, *plain), f32),
            pltpu.VMEM(plain, f32),
            pltpu.VMEM(plain, f32),
            pltpu.VMEM((2, max(X - 1, 1), q, NX, D), f32),
            pltpu.VMEM((2, max(Z - 1, 1), h, NX, D), f32),
            pltpu.VMEM((2, max(Y - 1, 1), h, c, D), f32),
            pltpu.VMEM((2, q, NX, D), f32),
            pltpu.VMEM((2, h, NX, D), f32),
            pltpu.VMEM((h + 2 * H, 3 * c, D), f32),
            pltpu.VMEM(plain, f32),
            pltpu.VMEM(plain, f32),
            pltpu.VMEM(plain, f32),
            pltpu.VMEM(plain, f32),
            pltpu.VMEM((3, *flat), f32),
            pltpu.SemaphoreType.DMA((5,)),
            pltpu.SemaphoreType.DMA((3,)),
            pltpu.SemaphoreType.DMA((8, 2)),
            pltpu.SemaphoreType.DMA((8, 2)),
            pltpu.SemaphoreType.DMA((2, n_rs)),
            pltpu.SemaphoreType.DMA((2, n_rs)),
            pltpu.SemaphoreType.DMA((n_rs,)),
            pltpu.SemaphoreType.DMA((n_rs,)),
            pltpu.SemaphoreType.DMA((n_near,)),
            pltpu.SemaphoreType.DMA((n_near,)),
        ],
        compiler_params=pltpu.CompilerParams(
            collective_id=0, has_side_effects=True, vmem_limit_bytes=56 * 1024 * 1024
        ),
    )(
        source_cell,
        wavelet,
        receiver_cell,
        residual.transpose(1, 0, 2),
        wave_prev.reshape(flat),
        wave_now.reshape(flat),
        adjoint_prev.reshape(flat),
        adjoint_now.reshape(flat),
        velocity.reshape(flat),
    )
    wave_out, adjoint_out, speed_out = pl.pallas_call(
        hand_over,
        out_shape=(out, out, out),
        in_specs=[anywhere] * 3,
        out_specs=(anywhere,) * 3,
        scratch_shapes=[pltpu.SemaphoreType.DMA((3,))],
    )(wave_out, adjoint_out, speed_out)
    field = (1, NX, R, D)
    return wave_out.reshape(field), adjoint_out.reshape(field), speed_out.reshape(field[1:])


def solution(mesh):
    shots, boxes = mesh.shape["shot"], mesh.shape["box"]
    parts = {64: (4, 2, 8), 16: (4, 2, 2), 8: (4, 2, 1)}[shots]
    return jax.shard_map(
        functools.partial(local, parts, boxes),
        mesh=mesh,
        in_specs=(
            P("shot", None, "box", None),
            P("shot", None, "box", None),
            P("shot", None, "box", None),
            P("shot", None, "box", None),
            P(None, "box", None),
            P("shot"),
            P("shot", None),
            P("shot", None),
            P("shot", None, None),
        ),
        out_specs=(
            P("shot", None, "box", None),
            P("shot", None, "box", None),
            P(None, "box", None),
        ),
        check_vma=False,
    )
```

```python
import functools

import jax
import jax.numpy as jnp
from jax import lax
from jax.experimental import pallas as pl
from jax.experimental.pallas import tpu as pltpu
from jax.sharding import PartitionSpec as P

MESH = pl.DeviceIdType.MESH
STEPS = 3
FINAL = 2
PASSES = 4
RDEPTH = 2
LANES = 128
H = 4
PAD = 8

stencil_weights = (-205.0 / 72.0, 8.0 / 5.0, -1.0 / 5.0, 8.0 / 315.0, -1.0 / 560.0)
diffuse_rate = 0.1
step_length = 0.1
speed_floor = 0.16
speed_ceiling = 0.44


def kernel(
    sizes,
    source_cell,
    wavelet,
    receiver_cell,
    residual,
    wave_prev,
    wave_now,
    adjoint_prev,
    adjoint_now,
    velocity,
    wave_out,
    adjoint_out,
    speed_out,
    staged,
    U,
    W,
    speed,
    square,
    received,
    G,
    I,
    rx,
    rp,
    sx,
    E,
    S,
    L,
    zu,
    zw,
    in_sem,
    halo_send,
    halo_recv,
    rs_send,
    rs_recv,
    ag_send,
    ag_recv,
    near_send,
    near_recv,
):
    X, Z, Y, boxes, NX, R = sizes
    NY = R * boxes
    q, h, c = R // X, R // (X * Z), NX // Y
    shot, box = lax.axis_index("shot"), lax.axis_index("box")
    x = lax.div(shot, Z * Y)
    z = lax.rem(lax.div(shot, Y), Z)
    y = lax.rem(shot, Y)
    lower, upper = lax.max(box - 1, 0), lax.min(box + 1, boxes - 1)
    has_lower, has_upper = box > 0, box < boxes - 1

    def peer_x(d):
        return (lax.rem(x + d, X) * Z + z) * Y + y

    def peer_zy(d, e):
        return (x * Z + lax.rem(z + d, Z)) * Y + lax.rem(y + e, Y)

    plane = [(d, e) for d in range(Z) for e in range(Y) if (d, e) != (0, 0)]

    pieces = X * Z
    place = box * pieces + x * Z + z
    reach = -(-H // h)
    beside = [e for e in (-1, 0, 1) if Y > 1 or e == 0]
    near = [(d, e) for d in range(-reach, reach + 1) for e in beside if (d, e) != (0, 0)]

    def is_near(d, e):
        return (place + d >= 0) & (place + d < boxes * pieces) & (y + e >= 0) & (y + e < Y)

    def owner(d, e):
        other = lax.clamp(0, place + d, boxes * pieces - 1)
        return {
            "shot": lax.rem(other, pieces) * Y + lax.clamp(0, y + e, Y - 1),
            "box": lax.div(other, pieces),
        }

    E[...] = jnp.zeros_like(E)

    loads = [
        pltpu.make_async_copy(ref, staged.at[i], in_sem.at[i])
        for i, ref in enumerate((wave_now, adjoint_now, wave_prev, adjoint_prev, velocity))
    ]
    for load in loads:
        load.start()

    barrier = pltpu.get_barrier_semaphore()
    peers = [peer_x(d) for d in range(1, X)] + [peer_zy(d, e) for d, e in plane]
    for peer in peers:
        pl.semaphore_signal(barrier, inc=1, device_id={"shot": peer}, device_id_type=MESH)

    @pl.when(has_lower)
    def _():
        pl.semaphore_signal(barrier, inc=1, device_id={"box": lower}, device_id_type=MESH)

    @pl.when(has_upper)
    def _():
        pl.semaphore_signal(barrier, inc=1, device_id={"box": upper}, device_id_type=MESH)

    count = len(peers) + has_lower.astype(jnp.int32) + has_upper.astype(jnp.int32)
    for d, e in near:

        @pl.when(is_near(d, e))
        def _(d=d, e=e):
            pl.semaphore_signal(barrier, inc=1, device_id=owner(d, e), device_id_type=MESH)

        count = count + is_near(d, e).astype(jnp.int32)

    pad = jnp.zeros((R, PAD, LANES), jnp.float32)
    edge = jnp.zeros((H, NX, LANES), jnp.float32)
    for fields, slots in ((U, range(1, 6)), (W, range(1, 4))):
        for slot in slots:
            fields[slot, H : H + R, :PAD, :] = pad
            fields[slot, H : H + R, PAD + NX :, :] = pad

    @pl.when(box == 0)
    def _():
        for fields, slots in ((U, range(1, 6)), (W, range(1, 4))):
            for slot in slots:
                fields[slot, :H, PAD : PAD + NX, :] = edge

    @pl.when(box == boxes - 1)
    def _():
        for fields, slots in ((U, range(1, 6)), (W, range(1, 4))):
            for slot in slots:
                fields[slot, H + R :, PAD : PAD + NX, :] = edge

    class Halo:
        def __init__(self, ref, index):
            def rows(start):
                return ref.at[pl.ds(start, H), pl.ds(PAD, NX), :]

            self.down = pltpu.make_async_remote_copy(
                src_ref=rows(H),
                dst_ref=rows(H + R),
                send_sem=halo_send.at[index, 0],
                recv_sem=halo_recv.at[index, 0],
                device_id={"box": lower},
                device_id_type=MESH,
            )
            self.up = pltpu.make_async_remote_copy(
                src_ref=rows(R),
                dst_ref=rows(0),
                send_sem=halo_send.at[index, 1],
                recv_sem=halo_recv.at[index, 1],
                device_id={"box": upper},
                device_id_type=MESH,
            )

        def start(self):
            pl.when(has_lower)(self.down.start)
            pl.when(has_upper)(self.up.start)

        def arrive(self):
            pl.when(has_lower)(self.up.wait_recv)
            pl.when(has_upper)(self.down.wait_recv)

        def leave(self):
            pl.when(has_lower)(self.down.wait_send)
            pl.when(has_upper)(self.up.wait_send)

    halo_u = {t: Halo(U.at[t], t - 1) for t in range(1, 6)}
    halo_w = {t: Halo(W.at[t], 4 + t) for t in range(1, 4)}

    lane = lax.broadcasted_iota(jnp.int32, (1, LANES), 1)
    first = lax.broadcasted_iota(jnp.int32, (NX, 1), 0)
    flat = lax.broadcasted_iota(jnp.int32, (NX, LANES), 0) * (NY * LANES) + lax.broadcasted_iota(
        jnp.int32, (NX, LANES), 1
    )
    start_second = box * R
    source = source_cell[0]

    def over(begin, end, body):
        lax.fori_loop(begin, end, lambda r, carry: (body(r), carry)[1], 0)

    def over_edges(body):
        def step(i, carry):
            body(jnp.where(i < H, i, i + (R - 2 * H)))
            return carry

        lax.fori_loop(0, 2 * H, step, 0)

    def turned(i, r):
        return staged[i, pl.ds(r, NX, stride=R), :]

    def centre(r):
        return (H + r, pl.ds(PAD, NX), slice(None))

    apart = lax.broadcasted_iota(jnp.int32, (LANES, LANES), 0) - lax.broadcasted_iota(
        jnp.int32, (LANES, LANES), 1
    )
    along_depth = jnp.where(apart == 0, 3.0 * stencil_weights[0], 0.0)
    for k in range(1, 5):
        along_depth = along_depth + jnp.where((apart == k) | (apart == -k), stencil_weights[k], 0.0)

    def depth(ref, out):
        field = ref[pl.ds(H, R), pl.ds(PAD, NX), :].reshape(R * NX, LANES)
        out[...] = lax.dot_general(
            field,
            along_depth,
            (((1,), (0,)), ((), ())),
            precision=lax.Precision.HIGHEST,
            preferred_element_type=jnp.float32,
        ).reshape(R, NX, LANES)

    def laplace(ref, along, r):
        summed = along[r]
        for k in range(1, 5):
            around = (ref[H + r + k, pl.ds(PAD, NX), :] + ref[H + r - k, pl.ds(PAD, NX), :]) + (
                ref[H + r, pl.ds(PAD + k, NX), :] + ref[H + r, pl.ds(PAD - k, NX), :]
            )
            summed = summed + stencil_weights[k] * around
        return summed

    def injected(r, amplitude):
        return jnp.where(flat == source - (start_second + r) * LANES, amplitude, 0.0)

    def wave_row(t):
        now, early, later = U.at[t], U.at[t - 1], U.at[t + 1]
        amplitude = wavelet[0, t - 1]

        def body(r):
            field = now[centre(r)]
            second_diff = square[r] * laplace(now, zu, r) + injected(r, amplitude)
            later[centre(r)] = (2.0 * field - early[centre(r)]) + second_diff
            term = W[(t, *centre(r))] * second_diff
            G[r] = term if t == 1 else G[r] + term

        return body

    def adjoint_row(t, last=False):
        now, early = W.at[t], W.at[t - 1]

        def body(r):
            value = (2.0 * now[centre(r)] - early[centre(r)]) + (
                square[r] * laplace(now, zw, r) + received[t - 1, r]
            )
            if last:
                adjoint_out[pl.ds(r, NX, stride=R), :] = value
            else:
                W[(t + 1, *centre(r))] = value

        return body

    pl.semaphore_wait(barrier, count)
    loads[0].wait()

    def turn_wave(r):
        U[(1, *centre(r))] = turned(0, r)

    over(0, R, turn_wave)
    halo_u[1].start()
    loads[1].wait()

    def turn_adjoint(r):
        W[(1, *centre(r))] = turned(1, r)

    over(0, R, turn_adjoint)
    depth(U.at[1], zu)
    loads[2].wait()
    loads[3].wait()
    loads[4].wait()

    def turn_rest(r):
        U[(0, *centre(r))] = turned(2, r)
        W[(0, *centre(r))] = turned(3, r)
        v = turned(4, r)
        speed[r] = v
        square[r] = v * v

    over(0, R, turn_rest)
    over(H, R - H, wave_row(1))

    def receive(t):
        shape = (R, NX, LANES)
        here = (
            lax.broadcasted_iota(jnp.int32, shape, 1) * NY
            + lax.broadcasted_iota(jnp.int32, shape, 0)
            + start_second
        ) * LANES + RDEPTH
        picks = jnp.where(here == receiver_cell[...].reshape(1, 1, LANES), 1.0, 0.0)
        picks = picks.astype(jnp.bfloat16).reshape(R * NX, LANES)
        at_depth = lax.broadcasted_iota(jnp.int32, (LANES, LANES), 0) == RDEPTH
        rest, total = jnp.where(at_depth, residual[t - 1], 0.0), None
        for _ in range(3):
            part = rest.astype(jnp.bfloat16)
            rest = rest - part.astype(jnp.float32)
            picked = lax.dot_general(
                picks, part, (((1,), (1,)), ((), ())), preferred_element_type=jnp.float32
            )
            total = picked if total is None else total + picked
        received[t - 1] = total.reshape(shape)

    receive(1)
    halo_u[1].leave()
    halo_w[1].start()
    depth(W.at[1], zw)


    class Reduce:
        def __init__(self, which, ref):
            self.ref, self.which = ref, which
            self.x = []
            for d in range(1, X):
                target = lax.rem(x + d, X)
                self.x.append(self.copy(d - 1, ref.at[pl.ds(target * q, q)], rx.at[which, d - 1], peer_x(d)))
            self.p = [
                self.copy(
                    X - 1 + i,
                    sx.at[
                        which,
                        pl.ds(lax.rem(z + d, Z) * h, h),
                        pl.ds(pl.multiple_of(lax.rem(y + e, Y) * c, c), c),
                        :,
                    ],
                    rp.at[which, i],
                    peer_zy(d, e),
                )
                for i, (d, e) in enumerate(plane)
            ]

        def copy(self, index, src, dst, peer):
            return pltpu.make_async_remote_copy(
                src_ref=src,
                dst_ref=dst,
                send_sem=rs_send.at[self.which, index],
                recv_sem=rs_recv.at[self.which, index],
                device_id={"shot": peer},
                device_id_type=MESH,
            )

        def start_x(self, part):
            d = lax.rem(part - x + X, X)

            @pl.when(d > 0)
            def _():
                slot = lax.max(d - 1, 0)
                self.copy(
                    slot, self.ref.at[pl.ds(part * q, q)], rx.at[self.which, slot], peer_x(d)
                ).start()

        def then_plane(self):
            for copy in self.x:
                copy.wait_recv()

            def add(r):
                total = self.ref[x * q + r]
                for d in range(1, X):
                    total = total + rx[self.which, d - 1, r]
                sx[self.which, r] = total

            over(0, q, add)
            for copy in self.p:
                copy.start()

        def piece(self):
            for copy in self.p:
                copy.wait_recv()
            total = sx[self.which, pl.ds(z * h, h), pl.ds(pl.multiple_of(y * c, c), c), :]
            for i in range(len(self.p)):
                total = total + rp[self.which, i]
            return total

        def leave(self):
            for copy in self.x + self.p:
                copy.wait_send()

    reduce_g, reduce_i = Reduce(0, G), Reduce(1, I)

    halo_u[1].arrive()
    over_edges(wave_row(1))
    halo_u[2].start()
    over(H, R - H, adjoint_row(1))
    receive(2)
    halo_w[1].arrive()
    over_edges(adjoint_row(1))
    halo_w[2].start()
    depth(U.at[2], zu)
    over(H, R - H, wave_row(2))
    halo_u[2].arrive()
    over_edges(wave_row(2))
    halo_u[3].start()
    depth(W.at[2], zw)
    over(H, R - H, adjoint_row(2))
    depth(U.at[3], zu)
    over(H, R - H, wave_row(3))
    for part in range(1, X - 1):
        reduce_g.start_x(part)

    def light(r):
        one, two, three = (U[(t, *centre(r))] for t in range(1, 4))
        I[r] = (one * one + two * two) + three * three

    over(0, R, light)
    for part in range(X):
        reduce_i.start_x(part)
    receive(3)
    halo_w[2].arrive()
    over_edges(adjoint_row(2))
    halo_u[3].arrive()
    over_edges(wave_row(3))
    for part in (0, X - 1):
        reduce_g.start_x(part)
    halo_u[4].start()
    halo_w[3].start()
    reduce_i.then_plane()
    depth(W.at[3], zw)
    over(H, R - H, adjoint_row(3, last=True))

    depth(U.at[STEPS + 1], zu)

    def before_update(r):
        L[r] = laplace(U.at[STEPS + 1], zu, r)
        U[(STEPS + 2, *centre(r))] = (
            2.0 * U[(STEPS + 1, *centre(r))] - U[(STEPS, *centre(r))]
        ) + injected(r, wavelet[0, STEPS])

    over(H, R - H, before_update)
    reduce_g.then_plane()
    illumination = reduce_i.piece()
    gradient = reduce_g.piece()

    E[pl.ds(H, h), pl.ds(c, c), :] = gradient / jnp.sqrt(illumination + 1.0)

    def index_of(d, e):
        return (d + reach) * 3 + e + 1

    def to_near(d, e):
        return pltpu.make_async_remote_copy(
            src_ref=E.at[pl.ds(H, h), pl.ds(c, c), :],
            dst_ref=E.at[pl.ds(H - d * h, h), pl.ds(c - e * c, c), :],
            send_sem=near_send.at[index_of(d, e)],
            recv_sem=near_recv.at[index_of(-d, -e)],
            device_id=owner(d, e),
            device_id_type=MESH,
        )

    for d, e in near:
        pl.when(is_near(d, e))(to_near(d, e).start)
    halo_u[STEPS + 1].arrive()
    over_edges(before_update)
    for d, e in near:
        pl.when(is_near(d, e))(to_near(-d, -e).wait_recv)

    row = x * q + z * h
    at_first = y * c - c + lax.broadcasted_iota(jnp.int32, (1, 3 * c, 1), 1)
    face_first = (at_first >= 0) & (at_first + 1 < NX)
    face_third = lax.broadcasted_iota(jnp.int32, (1, 1, LANES), 2) < LANES - 1

    def conduct(rise):
        return rise / (1.0 + rise * rise)

    smoothed = E[...]
    for turn in range(PASSES):
        rows = smoothed.shape[0]
        at_second = (start_second + row - H + turn + 1) + lax.broadcasted_iota(
            jnp.int32, (rows - 1, 1, 1), 0
        )
        face_second = (at_second > 0) & (at_second < NY)
        second = jnp.where(face_second, conduct(smoothed[1:] - smoothed[:-1]), 0.0)
        field = smoothed[1:-1]
        along_first = jnp.where(face_first, conduct(pltpu.roll(field, 3 * c - 1, 1) - field), 0.0)
        along_third = jnp.where(face_third, conduct(pltpu.roll(field, LANES - 1, 2) - field), 0.0)
        change = (
            (along_first - pltpu.roll(along_first, 1, 1))
            + (second[1:] - second[:-1])
            + (along_third - pltpu.roll(along_third, 1, 2))
        )
        smoothed = field + diffuse_rate * change
    mine = pl.ds(row, h), pl.ds(pl.multiple_of(y * c, c), c), slice(None)
    S[mine] = jnp.clip(speed[mine] - step_length * smoothed[:, c : 2 * c], speed_floor, speed_ceiling)

    def share(index, part, peer):
        return pltpu.make_async_remote_copy(
            src_ref=part,
            dst_ref=part,
            send_sem=ag_send.at[index],
            recv_sem=ag_recv.at[index],
            device_id={"shot": peer},
            device_id_type=MESH,
        )

    by_plane = [
        share(X - 1 + i, S.at[mine], peer_zy(d, e)) for i, (d, e) in enumerate(plane)
    ]
    for copy in by_plane:
        copy.start()
    halo_w[3].arrive()
    over_edges(adjoint_row(3, last=True))
    for copy in by_plane:
        copy.wait_recv()
    by_x = [share(d - 1, S.at[pl.ds(x * q, q)], peer_x(d)) for d in range(1, X)]

    def send_part():
        for copy in by_x:
            copy.start()

    inner = (x > 0) & (x < X - 1)
    pl.when(jnp.logical_not(inner))(send_part)

    def final_one(r):
        new_speed = S[r]
        speed_out[pl.ds(r, NX, stride=R), :] = new_speed
        new_square = new_speed * new_speed
        square[r] = new_square
        U[(STEPS + 2, *centre(r))] = U[(STEPS + 2, *centre(r))] + new_square * L[r]

    def final_two(r):
        wave_out[pl.ds(r, NX, stride=R), :] = (
            2.0 * U[(STEPS + 2, *centre(r))] - U[(STEPS + 1, *centre(r))]
        ) + (square[r] * laplace(U.at[STEPS + 2], zu, r) + injected(r, wavelet[0, STEPS + 1]))

    def part_of_first(part):
        d = lax.rem(x - part + X, X)

        @pl.when(d > 0)
        def _():
            share(lax.max(d - 1, 0), S.at[pl.ds(part * q, q)], peer_x(d)).wait_recv()

        over(part * q, part * q + q, final_one)

    for part in (0, X - 1):
        part_of_first(part)
    halo_u[STEPS + 2].start()
    pl.when(inner)(send_part)
    for part in range(1, X - 1):
        part_of_first(part)
    depth(U.at[STEPS + 2], zu)
    over(H, R - H, final_two)
    halo_u[STEPS + 2].arrive()
    over_edges(final_two)

    for halo in (*list(halo_u.values())[1:], *halo_w.values()):
        halo.leave()
    reduce_g.leave()
    reduce_i.leave()
    for d, e in near:
        pl.when(is_near(d, e))(to_near(d, e).wait_send)
    for copy in by_plane + by_x:
        copy.wait_send()


def hand_over(wave, adjoint, speed, wave_out, adjoint_out, speed_out, sem):
    copies = [
        pltpu.make_async_copy(src, dst, sem.at[i])
        for i, (src, dst) in enumerate(((wave, wave_out), (adjoint, adjoint_out), (speed, speed_out)))
    ]
    for copy in copies:
        copy.start()
    for copy in copies:
        copy.wait()


def local(
    parts,
    boxes,
    wave_prev,
    wave_now,
    adjoint_prev,
    adjoint_now,
    velocity,
    source_cell,
    wavelet,
    receiver_cell,
    residual,
):
    X, Z, Y = parts
    NX, R, D = velocity.shape
    q, h, c = R // X, R // (X * Z), NX // Y
    f32 = jnp.float32
    flat = (NX * R, D)
    padded = (R + 2 * H, NX + 2 * PAD, D)
    plain = (R, NX, D)
    n_rs = X + Z * Y - 2
    n_near = 3 * (2 * -(-H // h) + 1)
    vmem, smem, anywhere = (
        pl.BlockSpec(memory_space=pltpu.VMEM),
        pl.BlockSpec(memory_space=pltpu.SMEM),
        pl.BlockSpec(memory_space=pl.ANY),
    )
    out = jax.ShapeDtypeStruct(flat, f32)
    kept = pltpu.VMEM(flat, f32)
    wave_out, adjoint_out, speed_out = pl.pallas_call(
        functools.partial(kernel, (X, Z, Y, boxes, NX, R)),
        out_shape=(kept, kept, kept),
        in_specs=[smem, smem, vmem, vmem] + [anywhere] * 5,
        out_specs=(vmem, vmem, vmem),
        scratch_shapes=[
            pltpu.VMEM((5, *flat), f32),
            pltpu.VMEM((6, *padded), f32),
            pltpu.VMEM((4, *padded), f32),
            pltpu.VMEM(plain, f32),
            pltpu.VMEM(plain, f32),
            pltpu.VMEM((STEPS, *plain), f32),
            pltpu.VMEM(plain, f32),
            pltpu.VMEM(plain, f32),
            pltpu.VMEM((2, max(X - 1, 1), q, NX, D), f32),
            pltpu.VMEM((2, Z * Y - 1, h, c, D), f32),
            pltpu.VMEM((2, q, NX, D), f32),
            pltpu.VMEM((h + 2 * H, 3 * c, D), f32),
            pltpu.VMEM(plain, f32),
            pltpu.VMEM(plain, f32),
            pltpu.VMEM(plain, f32),
            pltpu.VMEM(plain, f32),
            pltpu.SemaphoreType.DMA((5,)),
            pltpu.SemaphoreType.DMA((8, 2)),
            pltpu.SemaphoreType.DMA((8, 2)),
            pltpu.SemaphoreType.DMA((2, n_rs)),
            pltpu.SemaphoreType.DMA((2, n_rs)),
            pltpu.SemaphoreType.DMA((n_rs,)),
            pltpu.SemaphoreType.DMA((n_rs,)),
            pltpu.SemaphoreType.DMA((n_near,)),
            pltpu.SemaphoreType.DMA((n_near,)),
        ],
        compiler_params=pltpu.CompilerParams(
            collective_id=0, has_side_effects=True, vmem_limit_bytes=56 * 1024 * 1024
        ),
    )(
        source_cell,
        wavelet,
        receiver_cell,
        residual.transpose(1, 0, 2),
        wave_prev.reshape(flat),
        wave_now.reshape(flat),
        adjoint_prev.reshape(flat),
        adjoint_now.reshape(flat),
        velocity.reshape(flat),
    )
    wave_out, adjoint_out, speed_out = pl.pallas_call(
        hand_over,
        out_shape=(out, out, out),
        in_specs=[vmem] * 3,
        out_specs=(anywhere,) * 3,
        scratch_shapes=[pltpu.SemaphoreType.DMA((3,))],
    )(*(pltpu.with_memory_space_constraint(a, pltpu.VMEM) for a in (wave_out, adjoint_out, speed_out)))
    field = (1, NX, R, D)
    return wave_out.reshape(field), adjoint_out.reshape(field), speed_out.reshape(field[1:])


def solution(mesh):
    shots, boxes = mesh.shape["shot"], mesh.shape["box"]
    parts = {64: (4, 2, 8), 16: (4, 2, 2), 8: (4, 2, 1)}[shots]
    return jax.shard_map(
        functools.partial(local, parts, boxes),
        mesh=mesh,
        in_specs=(
            P("shot", None, "box", None),
            P("shot", None, "box", None),
            P("shot", None, "box", None),
            P("shot", None, "box", None),
            P(None, "box", None),
            P("shot"),
            P("shot", None),
            P("shot", None),
            P("shot", None, None),
        ),
        out_specs=(
            P("shot", None, "box", None),
            P("shot", None, "box", None),
            P(None, "box", None),
        ),
        check_vma=False,
    )
```

```python
import functools

import jax
import jax.numpy as jnp
from jax import lax
from jax.experimental import pallas as pl
from jax.experimental.pallas import tpu as pltpu
from jax.sharding import PartitionSpec as P

MESH = pl.DeviceIdType.MESH
STEPS = 3
FINAL = 2
PASSES = 4
RDEPTH = 2
LANES = 128
H = 4
PAD = 8

stencil_weights = (-205.0 / 72.0, 8.0 / 5.0, -1.0 / 5.0, 8.0 / 315.0, -1.0 / 560.0)
diffuse_rate = 0.1
step_length = 0.1
speed_floor = 0.16
speed_ceiling = 0.44


def kernel(
    sizes,
    source_cell,
    wavelet,
    receiver_cell,
    residual,
    wave_prev,
    wave_now,
    adjoint_prev,
    adjoint_now,
    velocity,
    wave_out,
    adjoint_out,
    speed_out,
    staged,
    U,
    W,
    speed,
    square,
    received,
    G,
    I,
    rx,
    rp,
    sx,
    E,
    S,
    L,
    zu,
    zw,
    in_sem,
    halo_send,
    halo_recv,
    rs_send,
    rs_recv,
    ag_send,
    ag_recv,
    near_send,
    near_recv,
):
    X, Z, Y, boxes, NX, R = sizes
    NY = R * boxes
    h, c = R // (X * Z), NX // Y
    shot, box = lax.axis_index("shot"), lax.axis_index("box")
    x = lax.div(shot, Z * Y)
    z = lax.rem(lax.div(shot, Y), Z)
    y = lax.rem(shot, Y)
    lower, upper = lax.max(box - 1, 0), lax.min(box + 1, boxes - 1)
    has_lower, has_upper = box > 0, box < boxes - 1

    def peer_x(d):
        return (lax.rem(x + d, X) * Z + z) * Y + y

    def peer_zy(d, e):
        return (x * Z + lax.rem(z + d, Z)) * Y + lax.rem(y + e, Y)

    at_edge = (1, 7, 0, 6)
    in_middle = (2, 3, 4, 5)

    def chosen(index, table):
        value = table[0]
        for i in range(1, len(table)):
            value = jnp.where(index == i, table[i], value)
        return value

    def pair_of(x, z):
        return jnp.where(z == 0, chosen(x, at_edge), chosen(x, in_middle))

    plane = [(d, e) for d in range(Z) for e in range(Y) if (d, e) != (0, 0)]

    pieces = X * Z
    place = box * pieces + pair_of(x, z)
    reach = -(-H // h)
    beside = [e for e in (-1, 0, 1) if Y > 1 or e == 0]
    near = [(d, e) for d in range(-reach, reach + 1) for e in beside if (d, e) != (0, 0)]

    def is_near(d, e):
        return (place + d >= 0) & (place + d < boxes * pieces) & (y + e >= 0) & (y + e < Y)

    def owner(d, e):
        other = lax.clamp(0, place + d, boxes * pieces - 1)
        pair = lax.rem(other, pieces)
        to_x = chosen(pair, tuple((at_edge + in_middle).index(p) % X for p in range(pieces)))
        to_z = chosen(pair, tuple((at_edge + in_middle).index(p) // X for p in range(pieces)))
        return {
            "shot": (to_x * Z + to_z) * Y + lax.clamp(0, y + e, Y - 1),
            "box": lax.div(other, pieces),
        }

    E[...] = jnp.zeros_like(E)

    loads = [
        pltpu.make_async_copy(ref, staged.at[i], in_sem.at[i])
        for i, ref in enumerate((wave_now, adjoint_now, wave_prev, adjoint_prev, velocity))
    ]
    for load in loads:
        load.start()

    barrier = pltpu.get_barrier_semaphore()
    peers = [peer_x(d) for d in range(1, X)] + [peer_zy(d, e) for d, e in plane]
    for peer in peers:
        pl.semaphore_signal(barrier, inc=1, device_id={"shot": peer}, device_id_type=MESH)

    @pl.when(has_lower)
    def _():
        pl.semaphore_signal(barrier, inc=1, device_id={"box": lower}, device_id_type=MESH)

    @pl.when(has_upper)
    def _():
        pl.semaphore_signal(barrier, inc=1, device_id={"box": upper}, device_id_type=MESH)

    count = len(peers) + has_lower.astype(jnp.int32) + has_upper.astype(jnp.int32)
    for d, e in near:

        @pl.when(is_near(d, e))
        def _(d=d, e=e):
            pl.semaphore_signal(barrier, inc=1, device_id=owner(d, e), device_id_type=MESH)

        count = count + is_near(d, e).astype(jnp.int32)

    pad = jnp.zeros((R, PAD, LANES), jnp.float32)
    edge = jnp.zeros((H, NX, LANES), jnp.float32)
    for fields, slots in ((U, range(1, 6)), (W, range(1, 4))):
        for slot in slots:
            fields[slot, H : H + R, :PAD, :] = pad
            fields[slot, H : H + R, PAD + NX :, :] = pad

    @pl.when(box == 0)
    def _():
        for fields, slots in ((U, range(1, 6)), (W, range(1, 4))):
            for slot in slots:
                fields[slot, :H, PAD : PAD + NX, :] = edge

    @pl.when(box == boxes - 1)
    def _():
        for fields, slots in ((U, range(1, 6)), (W, range(1, 4))):
            for slot in slots:
                fields[slot, H + R :, PAD : PAD + NX, :] = edge

    class Halo:
        def __init__(self, ref, index):
            def rows(start):
                return ref.at[pl.ds(start, H), pl.ds(PAD, NX), :]

            self.down = pltpu.make_async_remote_copy(
                src_ref=rows(H),
                dst_ref=rows(H + R),
                send_sem=halo_send.at[index, 0],
                recv_sem=halo_recv.at[index, 0],
                device_id={"box": lower},
                device_id_type=MESH,
            )
            self.up = pltpu.make_async_remote_copy(
                src_ref=rows(R),
                dst_ref=rows(0),
                send_sem=halo_send.at[index, 1],
                recv_sem=halo_recv.at[index, 1],
                device_id={"box": upper},
                device_id_type=MESH,
            )

        def start(self):
            pl.when(has_lower)(self.down.start)
            pl.when(has_upper)(self.up.start)

        def arrive(self):
            pl.when(has_lower)(self.up.wait_recv)
            pl.when(has_upper)(self.down.wait_recv)

        def leave(self):
            pl.when(has_lower)(self.down.wait_send)
            pl.when(has_upper)(self.up.wait_send)

    halo_u = {t: Halo(U.at[t], t - 1) for t in range(1, 6)}
    halo_w = {t: Halo(W.at[t], 4 + t) for t in range(1, 4)}

    lane = lax.broadcasted_iota(jnp.int32, (1, LANES), 1)
    first = lax.broadcasted_iota(jnp.int32, (NX, 1), 0)
    flat = lax.broadcasted_iota(jnp.int32, (NX, LANES), 0) * (NY * LANES) + lax.broadcasted_iota(
        jnp.int32, (NX, LANES), 1
    )
    start_second = box * R
    source = source_cell[0]

    def over(begin, end, body):
        lax.fori_loop(begin, end, lambda r, carry: (body(r), carry)[1], 0)

    def over_edges(body):
        def step(i, carry):
            body(jnp.where(i < H, i, i + (R - 2 * H)))
            return carry

        lax.fori_loop(0, 2 * H, step, 0)

    def turned(i, r):
        return staged[i, pl.ds(r, NX, stride=R), :]

    def centre(r):
        return (H + r, pl.ds(PAD, NX), slice(None))

    apart = lax.broadcasted_iota(jnp.int32, (LANES, LANES), 0) - lax.broadcasted_iota(
        jnp.int32, (LANES, LANES), 1
    )
    along_depth = jnp.where(apart == 0, 3.0 * stencil_weights[0], 0.0)
    for k in range(1, 5):
        along_depth = along_depth + jnp.where((apart == k) | (apart == -k), stencil_weights[k], 0.0)

    def depth(ref, out):
        field = ref[pl.ds(H, R), pl.ds(PAD, NX), :].reshape(R * NX, LANES)
        out[...] = lax.dot_general(
            field,
            along_depth,
            (((1,), (0,)), ((), ())),
            precision=lax.Precision.HIGHEST,
            preferred_element_type=jnp.float32,
        ).reshape(R, NX, LANES)

    def laplace(ref, along, r):
        summed = along[r]
        for k in range(1, 5):
            around = (ref[H + r + k, pl.ds(PAD, NX), :] + ref[H + r - k, pl.ds(PAD, NX), :]) + (
                ref[H + r, pl.ds(PAD + k, NX), :] + ref[H + r, pl.ds(PAD - k, NX), :]
            )
            summed = summed + stencil_weights[k] * around
        return summed

    def injected(r, amplitude):
        return jnp.where(flat == source - (start_second + r) * LANES, amplitude, 0.0)

    def wave_row(t):
        now, early, later = U.at[t], U.at[t - 1], U.at[t + 1]
        amplitude = wavelet[0, t - 1]

        def body(r):
            field = now[centre(r)]
            second_diff = square[r] * laplace(now, zu, r) + injected(r, amplitude)
            later[centre(r)] = (2.0 * field - early[centre(r)]) + second_diff
            term = W[(t, *centre(r))] * second_diff
            G[r] = term if t == 1 else G[r] + term

        return body

    def adjoint_row(t, last=False):
        now, early = W.at[t], W.at[t - 1]

        def body(r):
            value = (2.0 * now[centre(r)] - early[centre(r)]) + (
                square[r] * laplace(now, zw, r) + received[t - 1, r]
            )
            if last:
                adjoint_out[pl.ds(r, NX, stride=R), :] = value
            else:
                W[(t + 1, *centre(r))] = value

        return body

    pl.semaphore_wait(barrier, count)
    loads[0].wait()

    def turn_wave(r):
        U[(1, *centre(r))] = turned(0, r)

    over(0, R, turn_wave)
    halo_u[1].start()
    loads[1].wait()

    def turn_adjoint(r):
        W[(1, *centre(r))] = turned(1, r)

    over(0, R, turn_adjoint)
    depth(U.at[1], zu)
    loads[2].wait()
    loads[3].wait()
    loads[4].wait()

    def turn_rest(r):
        U[(0, *centre(r))] = turned(2, r)
        W[(0, *centre(r))] = turned(3, r)
        v = turned(4, r)
        speed[r] = v
        square[r] = v * v

    over(0, R, turn_rest)
    over(H, R - H, wave_row(1))

    def receive(t):
        shape = (R, NX, LANES)
        here = (
            lax.broadcasted_iota(jnp.int32, shape, 1) * NY
            + lax.broadcasted_iota(jnp.int32, shape, 0)
            + start_second
        ) * LANES + RDEPTH
        picks = jnp.where(here == receiver_cell[...].reshape(1, 1, LANES), 1.0, 0.0)
        picks = picks.astype(jnp.bfloat16).reshape(R * NX, LANES)
        at_depth = lax.broadcasted_iota(jnp.int32, (LANES, LANES), 0) == RDEPTH
        rest, total = jnp.where(at_depth, residual[t - 1], 0.0), None
        for _ in range(3):
            part = rest.astype(jnp.bfloat16)
            rest = rest - part.astype(jnp.float32)
            picked = lax.dot_general(
                picks, part, (((1,), (1,)), ((), ())), preferred_element_type=jnp.float32
            )
            total = picked if total is None else total + picked
        received[t - 1] = total.reshape(shape)

    receive(1)
    halo_u[1].leave()
    halo_w[1].start()
    depth(W.at[1], zw)


    class Reduce:
        def __init__(self, which, ref):
            self.ref, self.which = ref, which
            self.x = [
                [
                    self.copy(k * (X - 1) + d - 1, ref.at[pl.ds(0, h)], rx.at[which, k, d - 1], peer_x(d))
                    for d in range(1, X)
                ]
                for k in range(Z)
            ]
            self.p = [
                self.copy(Z * (X - 1) + i, ref.at[pl.ds(0, h), pl.ds(0, c), :], rp.at[which, i], peer_zy(d, e))
                for i, (d, e) in enumerate(plane)
            ]

        def copy(self, index, src, dst, peer):
            return pltpu.make_async_remote_copy(
                src_ref=src,
                dst_ref=dst,
                send_sem=rs_send.at[self.which, index],
                recv_sem=rs_recv.at[self.which, index],
                device_id={"shot": peer},
                device_id_type=MESH,
            )

        def start_x(self, k):
            for to in range(X):
                d = lax.rem(to - x + X, X)
                slot = lax.max(d - 1, 0)
                begin = h * (at_edge, in_middle)[k][to]
                copy = self.copy(
                    k * (X - 1) + slot, self.ref.at[pl.ds(begin, h)], rx.at[self.which, k, slot], peer_x(d)
                )
                pl.when(d > 0)(copy.start)

        def then_plane(self, k):
            for copy in self.x[k]:
                copy.wait_recv()
            begin = h * chosen(x, (at_edge, in_middle)[k])
            for r in range(h):
                total = self.ref[begin + r]
                for d in range(1, X):
                    total = total + rx[self.which, k, d - 1, r]
                sx[self.which, k * h + r] = total
            d = lax.rem(k - z + Z, Z)
            for e in range(Y):
                slot = d * Y + e - 1 if e > 0 else lax.max(d * Y - 1, 0)
                copy = self.copy(
                    Z * (X - 1) + slot,
                    sx.at[
                        self.which,
                        pl.ds(k * h, h),
                        pl.ds(pl.multiple_of(lax.rem(y + e, Y) * c, c), c),
                        :,
                    ],
                    rp.at[self.which, slot],
                    peer_zy(d, e),
                )
                if e > 0:
                    copy.start()
                else:
                    pl.when(d > 0)(copy.start)

        def piece(self):
            for copy in self.p:
                copy.wait_recv()
            total = sx[self.which, pl.ds(z * h, h), pl.ds(pl.multiple_of(y * c, c), c), :]
            for i in range(len(self.p)):
                total = total + rp[self.which, i]
            return total

        def leave(self):
            for copy in sum(self.x, []) + self.p:
                copy.wait_send()

    reduce_g, reduce_i = Reduce(0, G), Reduce(1, I)

    halo_u[1].arrive()
    over_edges(wave_row(1))
    halo_u[2].start()
    over(H, R - H, adjoint_row(1))
    receive(2)
    halo_w[1].arrive()
    over_edges(adjoint_row(1))
    halo_w[2].start()
    depth(U.at[2], zu)
    over(H, R - H, wave_row(2))
    halo_u[2].arrive()
    over_edges(wave_row(2))
    halo_u[3].start()
    depth(W.at[2], zw)
    over(H, R - H, adjoint_row(2))
    depth(U.at[3], zu)
    over(H, R - H, wave_row(3))
    reduce_g.start_x(1)

    def light(r):
        one, two, three = (U[(t, *centre(r))] for t in range(1, 4))
        I[r] = (one * one + two * two) + three * three

    over(0, R, light)
    reduce_i.start_x(1)
    reduce_i.start_x(0)
    receive(3)
    halo_w[2].arrive()
    over_edges(adjoint_row(2))
    halo_u[3].arrive()
    over_edges(wave_row(3))
    reduce_g.start_x(0)
    halo_u[4].start()
    reduce_g.then_plane(1)
    halo_w[3].start()
    reduce_i.then_plane(1)
    reduce_i.then_plane(0)
    depth(W.at[3], zw)
    over(H, R - H, adjoint_row(3, last=True))

    depth(U.at[STEPS + 1], zu)

    def before_update(r):
        L[r] = laplace(U.at[STEPS + 1], zu, r)
        U[(STEPS + 2, *centre(r))] = (
            2.0 * U[(STEPS + 1, *centre(r))] - U[(STEPS, *centre(r))]
        ) + injected(r, wavelet[0, STEPS])

    over(H, R - H, before_update)
    reduce_g.then_plane(0)
    illumination = reduce_i.piece()
    gradient = reduce_g.piece()

    E[pl.ds(H, h), pl.ds(c, c), :] = gradient / jnp.sqrt(illumination + 1.0)

    def index_of(d, e):
        return (d + reach) * 3 + e + 1

    def to_near(d, e):
        return pltpu.make_async_remote_copy(
            src_ref=E.at[pl.ds(H, h), pl.ds(c, c), :],
            dst_ref=E.at[pl.ds(H - d * h, h), pl.ds(c - e * c, c), :],
            send_sem=near_send.at[index_of(d, e)],
            recv_sem=near_recv.at[index_of(-d, -e)],
            device_id=owner(d, e),
            device_id_type=MESH,
        )

    for d, e in near:
        pl.when(is_near(d, e))(to_near(d, e).start)
    halo_u[STEPS + 1].arrive()
    over_edges(before_update)
    for d, e in near:
        pl.when(is_near(d, e))(to_near(-d, -e).wait_recv)

    row = h * pair_of(x, z)
    at_first = y * c - c + lax.broadcasted_iota(jnp.int32, (1, 3 * c, 1), 1)
    face_first = (at_first >= 0) & (at_first + 1 < NX)
    face_third = lax.broadcasted_iota(jnp.int32, (1, 1, LANES), 2) < LANES - 1

    def conduct(rise):
        return rise / (1.0 + rise * rise)

    smoothed = E[...]
    for turn in range(PASSES):
        rows = smoothed.shape[0]
        at_second = (start_second + row - H + turn + 1) + lax.broadcasted_iota(
            jnp.int32, (rows - 1, 1, 1), 0
        )
        face_second = (at_second > 0) & (at_second < NY)
        second = jnp.where(face_second, conduct(smoothed[1:] - smoothed[:-1]), 0.0)
        field = smoothed[1:-1]
        along_first = jnp.where(face_first, conduct(pltpu.roll(field, 3 * c - 1, 1) - field), 0.0)
        along_third = jnp.where(face_third, conduct(pltpu.roll(field, LANES - 1, 2) - field), 0.0)
        change = (
            (along_first - pltpu.roll(along_first, 1, 1))
            + (second[1:] - second[:-1])
            + (along_third - pltpu.roll(along_third, 1, 2))
        )
        smoothed = field + diffuse_rate * change
    mine = pl.ds(row, h), pl.ds(pl.multiple_of(y * c, c), c), slice(None)
    S[mine] = jnp.clip(speed[mine] - step_length * smoothed[:, c : 2 * c], speed_floor, speed_ceiling)

    def share(index, part, peer):
        return pltpu.make_async_remote_copy(
            src_ref=part,
            dst_ref=part,
            send_sem=ag_send.at[index],
            recv_sem=ag_recv.at[index],
            device_id={"shot": peer},
            device_id_type=MESH,
        )

    first_slot = Z * (X - 1)
    by_plane = [
        share(first_slot + i, S.at[mine], peer_zy(d, e)) for i, (d, e) in enumerate(plane)
    ]
    for copy in by_plane:
        copy.start()
    halo_w[3].arrive()
    over_edges(adjoint_row(3, last=True))
    by_x = []
    for k in range(Z):
        d = lax.rem(z - k + Z, Z)
        for e in range(Y):
            slot = first_slot + (d * Y + e - 1 if e > 0 else lax.max(d * Y - 1, 0))
            if e > 0:
                share(slot, S.at[mine], peer_zy(d, e)).wait_recv()
            else:
                pl.when(d > 0)(share(slot, S.at[mine], peer_zy(d, e)).wait_recv)
        part = S.at[pl.ds(h * chosen(x, (at_edge, in_middle)[k]), h)]
        by_x.append([share(k * (X - 1) + d - 1, part, peer_x(d)) for d in range(1, X)])
        for copy in by_x[k]:
            copy.start()

    def final_one(r):
        new_speed = S[r]
        speed_out[pl.ds(r, NX, stride=R), :] = new_speed
        new_square = new_speed * new_speed
        square[r] = new_square
        U[(STEPS + 2, *centre(r))] = U[(STEPS + 2, *centre(r))] + new_square * L[r]

    def final_two(r):
        wave_out[pl.ds(r, NX, stride=R), :] = (
            2.0 * U[(STEPS + 2, *centre(r))] - U[(STEPS + 1, *centre(r))]
        ) + (square[r] * laplace(U.at[STEPS + 2], zu, r) + injected(r, wavelet[0, STEPS + 1]))

    for copy in by_x[0]:
        copy.wait_recv()
    over_edges(final_one)
    halo_u[STEPS + 2].start()
    for copy in by_x[1]:
        copy.wait_recv()
    over(H, R - H, final_one)
    depth(U.at[STEPS + 2], zu)
    over(H, R - H, final_two)
    halo_u[STEPS + 2].arrive()
    over_edges(final_two)

    for halo in (*list(halo_u.values())[1:], *halo_w.values()):
        halo.leave()
    reduce_g.leave()
    reduce_i.leave()
    for d, e in near:
        pl.when(is_near(d, e))(to_near(d, e).wait_send)
    for copy in by_plane + sum(by_x, []):
        copy.wait_send()


def hand_over(wave, adjoint, speed, wave_out, adjoint_out, speed_out, sem):
    copies = [
        pltpu.make_async_copy(src, dst, sem.at[i])
        for i, (src, dst) in enumerate(((wave, wave_out), (adjoint, adjoint_out), (speed, speed_out)))
    ]
    for copy in copies:
        copy.start()
    for copy in copies:
        copy.wait()


def local(
    parts,
    boxes,
    wave_prev,
    wave_now,
    adjoint_prev,
    adjoint_now,
    velocity,
    source_cell,
    wavelet,
    receiver_cell,
    residual,
):
    X, Z, Y = parts
    NX, R, D = velocity.shape
    q, h, c = R // X, R // (X * Z), NX // Y
    f32 = jnp.float32
    flat = (NX * R, D)
    padded = (R + 2 * H, NX + 2 * PAD, D)
    plain = (R, NX, D)
    n_rs = Z * (X - 1) + Z * Y - 1
    n_near = 3 * (2 * -(-H // h) + 1)
    vmem, smem, anywhere = (
        pl.BlockSpec(memory_space=pltpu.VMEM),
        pl.BlockSpec(memory_space=pltpu.SMEM),
        pl.BlockSpec(memory_space=pl.ANY),
    )
    out = jax.ShapeDtypeStruct(flat, f32)
    kept = pltpu.VMEM(flat, f32)
    wave_out, adjoint_out, speed_out = pl.pallas_call(
        functools.partial(kernel, (X, Z, Y, boxes, NX, R)),
        out_shape=(kept, kept, kept),
        in_specs=[smem, smem, vmem, vmem] + [anywhere] * 5,
        out_specs=(vmem, vmem, vmem),
        scratch_shapes=[
            pltpu.VMEM((5, *flat), f32),
            pltpu.VMEM((6, *padded), f32),
            pltpu.VMEM((4, *padded), f32),
            pltpu.VMEM(plain, f32),
            pltpu.VMEM(plain, f32),
            pltpu.VMEM((STEPS, *plain), f32),
            pltpu.VMEM(plain, f32),
            pltpu.VMEM(plain, f32),
            pltpu.VMEM((2, Z, X - 1, h, NX, D), f32),
            pltpu.VMEM((2, Z * Y - 1, h, c, D), f32),
            pltpu.VMEM((2, q, NX, D), f32),
            pltpu.VMEM((h + 2 * H, 3 * c, D), f32),
            pltpu.VMEM(plain, f32),
            pltpu.VMEM(plain, f32),
            pltpu.VMEM(plain, f32),
            pltpu.VMEM(plain, f32),
            pltpu.SemaphoreType.DMA((5,)),
            pltpu.SemaphoreType.DMA((8, 2)),
            pltpu.SemaphoreType.DMA((8, 2)),
            pltpu.SemaphoreType.DMA((2, n_rs)),
            pltpu.SemaphoreType.DMA((2, n_rs)),
            pltpu.SemaphoreType.DMA((n_rs,)),
            pltpu.SemaphoreType.DMA((n_rs,)),
            pltpu.SemaphoreType.DMA((n_near,)),
            pltpu.SemaphoreType.DMA((n_near,)),
        ],
        compiler_params=pltpu.CompilerParams(
            collective_id=0, has_side_effects=True, vmem_limit_bytes=56 * 1024 * 1024
        ),
    )(
        source_cell,
        wavelet,
        receiver_cell,
        residual.transpose(1, 0, 2),
        wave_prev.reshape(flat),
        wave_now.reshape(flat),
        adjoint_prev.reshape(flat),
        adjoint_now.reshape(flat),
        velocity.reshape(flat),
    )
    wave_out, adjoint_out, speed_out = pl.pallas_call(
        hand_over,
        out_shape=(out, out, out),
        in_specs=[vmem] * 3,
        out_specs=(anywhere,) * 3,
        scratch_shapes=[pltpu.SemaphoreType.DMA((3,))],
    )(*(pltpu.with_memory_space_constraint(a, pltpu.VMEM) for a in (wave_out, adjoint_out, speed_out)))
    field = (1, NX, R, D)
    return wave_out.reshape(field), adjoint_out.reshape(field), speed_out.reshape(field[1:])


def solution(mesh):
    shots, boxes = mesh.shape["shot"], mesh.shape["box"]
    parts = {64: (4, 2, 8), 16: (4, 2, 2), 8: (4, 2, 1)}[shots]
    return jax.shard_map(
        functools.partial(local, parts, boxes),
        mesh=mesh,
        in_specs=(
            P("shot", None, "box", None),
            P("shot", None, "box", None),
            P("shot", None, "box", None),
            P("shot", None, "box", None),
            P(None, "box", None),
            P("shot"),
            P("shot", None),
            P("shot", None),
            P("shot", None, None),
        ),
        out_specs=(
            P("shot", None, "box", None),
            P("shot", None, "box", None),
            P(None, "box", None),
        ),
        check_vma=False,
    )
```

```python
import functools

import jax
import jax.numpy as jnp
from jax import lax
from jax.experimental import pallas as pl
from jax.experimental.pallas import tpu as pltpu
from jax.sharding import PartitionSpec as P

MESH = pl.DeviceIdType.MESH
STEPS = 3
FINAL = 2
PASSES = 4
RDEPTH = 2
LANES = 128
H = 4
PAD = 8

stencil_weights = (-205.0 / 72.0, 8.0 / 5.0, -1.0 / 5.0, 8.0 / 315.0, -1.0 / 560.0)
diffuse_rate = 0.1
step_length = 0.1
speed_floor = 0.16
speed_ceiling = 0.44


def kernel(
    sizes,
    source_cell,
    wavelet,
    receiver_cell,
    residual,
    wave_prev,
    wave_now,
    adjoint_prev,
    adjoint_now,
    velocity,
    wave_out,
    adjoint_out,
    speed_out,
    staged,
    U,
    W,
    speed,
    square,
    received,
    G,
    I,
    rx,
    rp,
    sx,
    E,
    S,
    L,
    zu,
    zw,
    in_sem,
    halo_send,
    halo_recv,
    rs_send,
    rs_recv,
    ag_send,
    ag_recv,
    near_send,
    near_recv,
):
    X, Z, Y, boxes, NX, R = sizes
    NY = R * boxes
    h, c = R // (X * Z), NX // Y
    shot, box = lax.axis_index("shot"), lax.axis_index("box")
    x = lax.div(shot, Z * Y)
    z = lax.rem(lax.div(shot, Y), Z)
    y = lax.rem(shot, Y)
    lower, upper = lax.max(box - 1, 0), lax.min(box + 1, boxes - 1)
    has_lower, has_upper = box > 0, box < boxes - 1

    def peer_x(d):
        return (lax.rem(x + d, X) * Z + z) * Y + y

    def peer_zy(d, e):
        return (x * Z + lax.rem(z + d, Z)) * Y + lax.rem(y + e, Y)

    at_edge = (1, 7, 0, 6)
    in_middle = (2, 3, 4, 5)

    def chosen(index, table):
        value = table[0]
        for i in range(1, len(table)):
            value = jnp.where(index == i, table[i], value)
        return value

    def pair_of(x, z):
        return jnp.where(z == 0, chosen(x, at_edge), chosen(x, in_middle))

    plane = [(d, e) for d in range(Z) for e in range(Y) if (d, e) != (0, 0)]

    pieces = X * Z
    place = box * pieces + pair_of(x, z)
    reach = -(-H // h)
    beside = [e for e in (-1, 0, 1) if Y > 1 or e == 0]
    near = [(d, e) for d in range(-reach, reach + 1) for e in beside if (d, e) != (0, 0)]

    def is_near(d, e):
        return (place + d >= 0) & (place + d < boxes * pieces) & (y + e >= 0) & (y + e < Y)

    def owner(d, e):
        other = lax.clamp(0, place + d, boxes * pieces - 1)
        pair = lax.rem(other, pieces)
        to_x = chosen(pair, tuple((at_edge + in_middle).index(p) % X for p in range(pieces)))
        to_z = chosen(pair, tuple((at_edge + in_middle).index(p) // X for p in range(pieces)))
        return {
            "shot": (to_x * Z + to_z) * Y + lax.clamp(0, y + e, Y - 1),
            "box": lax.div(other, pieces),
        }

    E[...] = jnp.zeros_like(E)

    loads = [
        pltpu.make_async_copy(ref, staged.at[i], in_sem.at[i])
        for i, ref in enumerate((wave_now, adjoint_now, wave_prev, adjoint_prev, velocity))
    ]
    for load in loads:
        load.start()

    barrier = pltpu.get_barrier_semaphore()
    peers = [peer_x(d) for d in range(1, X)] + [peer_zy(d, e) for d, e in plane]
    for peer in peers:
        pl.semaphore_signal(barrier, inc=1, device_id={"shot": peer}, device_id_type=MESH)

    @pl.when(has_lower)
    def _():
        pl.semaphore_signal(barrier, inc=1, device_id={"box": lower}, device_id_type=MESH)

    @pl.when(has_upper)
    def _():
        pl.semaphore_signal(barrier, inc=1, device_id={"box": upper}, device_id_type=MESH)

    count = len(peers) + has_lower.astype(jnp.int32) + has_upper.astype(jnp.int32)
    for d, e in near:

        @pl.when(is_near(d, e))
        def _(d=d, e=e):
            pl.semaphore_signal(barrier, inc=1, device_id=owner(d, e), device_id_type=MESH)

        count = count + is_near(d, e).astype(jnp.int32)

    pad = jnp.zeros((R, PAD, LANES), jnp.float32)
    edge = jnp.zeros((H, NX, LANES), jnp.float32)
    for fields, slots in ((U, range(1, 6)), (W, range(1, 4))):
        for slot in slots:
            fields[slot, H : H + R, :PAD, :] = pad
            fields[slot, H : H + R, PAD + NX :, :] = pad

    @pl.when(box == 0)
    def _():
        for fields, slots in ((U, range(1, 6)), (W, range(1, 4))):
            for slot in slots:
                fields[slot, :H, PAD : PAD + NX, :] = edge

    @pl.when(box == boxes - 1)
    def _():
        for fields, slots in ((U, range(1, 6)), (W, range(1, 4))):
            for slot in slots:
                fields[slot, H + R :, PAD : PAD + NX, :] = edge

    class Halo:
        def __init__(self, ref, index):
            def rows(start):
                return ref.at[pl.ds(start, H), pl.ds(PAD, NX), :]

            self.down = pltpu.make_async_remote_copy(
                src_ref=rows(H),
                dst_ref=rows(H + R),
                send_sem=halo_send.at[index, 0],
                recv_sem=halo_recv.at[index, 0],
                device_id={"box": lower},
                device_id_type=MESH,
            )
            self.up = pltpu.make_async_remote_copy(
                src_ref=rows(R),
                dst_ref=rows(0),
                send_sem=halo_send.at[index, 1],
                recv_sem=halo_recv.at[index, 1],
                device_id={"box": upper},
                device_id_type=MESH,
            )

        def start(self):
            pl.when(has_lower)(self.down.start)
            pl.when(has_upper)(self.up.start)

        def arrive(self):
            pl.when(has_lower)(self.up.wait_recv)
            pl.when(has_upper)(self.down.wait_recv)

        def leave(self):
            pl.when(has_lower)(self.down.wait_send)
            pl.when(has_upper)(self.up.wait_send)

    halo_u = {t: Halo(U.at[t], t - 1) for t in range(1, 6)}
    halo_w = {t: Halo(W.at[t], 4 + t) for t in range(1, 4)}

    lane = lax.broadcasted_iota(jnp.int32, (1, LANES), 1)
    first = lax.broadcasted_iota(jnp.int32, (NX, 1), 0)
    flat = lax.broadcasted_iota(jnp.int32, (NX, LANES), 0) * (NY * LANES) + lax.broadcasted_iota(
        jnp.int32, (NX, LANES), 1
    )
    start_second = box * R
    source = source_cell[0]

    def over(begin, end, body):
        lax.fori_loop(begin, end, lambda r, carry: (body(r), carry)[1], 0)

    def over_edges(body):
        def step(i, carry):
            body(jnp.where(i < H, i, i + (R - 2 * H)))
            return carry

        lax.fori_loop(0, 2 * H, step, 0)

    def turned(i, r):
        return staged[i, pl.ds(r, NX, stride=R), :]

    def centre(r):
        return (H + r, pl.ds(PAD, NX), slice(None))

    apart = lax.broadcasted_iota(jnp.int32, (LANES, LANES), 0) - lax.broadcasted_iota(
        jnp.int32, (LANES, LANES), 1
    )
    along_depth = jnp.where(apart == 0, 3.0 * stencil_weights[0], 0.0)
    for k in range(1, 5):
        along_depth = along_depth + jnp.where((apart == k) | (apart == -k), stencil_weights[k], 0.0)

    def depth(ref, out):
        field = ref[pl.ds(H, R), pl.ds(PAD, NX), :].reshape(R * NX, LANES)
        out[...] = lax.dot_general(
            field,
            along_depth,
            (((1,), (0,)), ((), ())),
            precision=lax.Precision.HIGHEST,
            preferred_element_type=jnp.float32,
        ).reshape(R, NX, LANES)

    def laplace(ref, along, r):
        summed = along[r]
        for k in range(1, 5):
            around = (ref[H + r + k, pl.ds(PAD, NX), :] + ref[H + r - k, pl.ds(PAD, NX), :]) + (
                ref[H + r, pl.ds(PAD + k, NX), :] + ref[H + r, pl.ds(PAD - k, NX), :]
            )
            summed = summed + stencil_weights[k] * around
        return summed

    def injected(r, amplitude):
        return jnp.where(flat == source - (start_second + r) * LANES, amplitude, 0.0)

    def wave_row(t):
        now, early, later = U.at[t], U.at[t - 1], U.at[t + 1]
        amplitude = wavelet[0, t - 1]

        def body(r):
            field = now[centre(r)]
            second_diff = square[r] * laplace(now, zu, r) + injected(r, amplitude)
            later[centre(r)] = (2.0 * field - early[centre(r)]) + second_diff
            term = W[(t, *centre(r))] * second_diff
            G[r] = term if t == 1 else G[r] + term

        return body

    def adjoint_row(t, last=False):
        now, early = W.at[t], W.at[t - 1]

        def body(r):
            value = (2.0 * now[centre(r)] - early[centre(r)]) + (
                square[r] * laplace(now, zw, r) + received[t - 1, r]
            )
            if last:
                adjoint_out[pl.ds(r, NX, stride=R), :] = value
            else:
                W[(t + 1, *centre(r))] = value

        return body

    loads[0].wait()

    def turn_wave(r):
        U[(1, *centre(r))] = turned(0, r)

    over(0, R, turn_wave)
    pl.semaphore_wait(barrier, count)
    halo_u[1].start()
    loads[1].wait()

    def turn_adjoint(r):
        W[(1, *centre(r))] = turned(1, r)

    over(0, R, turn_adjoint)
    depth(U.at[1], zu)
    loads[2].wait()
    loads[3].wait()
    loads[4].wait()

    def turn_rest(r):
        U[(0, *centre(r))] = turned(2, r)
        W[(0, *centre(r))] = turned(3, r)
        v = turned(4, r)
        speed[r] = v
        square[r] = v * v

    over(0, R, turn_rest)
    over(H, R - H, wave_row(1))

    def receive(t):
        shape = (R, NX, LANES)
        here = (
            lax.broadcasted_iota(jnp.int32, shape, 1) * NY
            + lax.broadcasted_iota(jnp.int32, shape, 0)
            + start_second
        ) * LANES + RDEPTH
        picks = jnp.where(here == receiver_cell[...].reshape(1, 1, LANES), 1.0, 0.0)
        picks = picks.astype(jnp.bfloat16).reshape(R * NX, LANES)
        at_depth = lax.broadcasted_iota(jnp.int32, (LANES, LANES), 0) == RDEPTH
        rest, total = jnp.where(at_depth, residual[t - 1], 0.0), None
        for _ in range(3):
            part = rest.astype(jnp.bfloat16)
            rest = rest - part.astype(jnp.float32)
            picked = lax.dot_general(
                picks, part, (((1,), (1,)), ((), ())), preferred_element_type=jnp.float32
            )
            total = picked if total is None else total + picked
        received[t - 1] = total.reshape(shape)

    receive(1)
    halo_u[1].leave()
    halo_w[1].start()
    depth(W.at[1], zw)


    class Reduce:
        def __init__(self, which, ref):
            self.ref, self.which = ref, which
            self.x = [
                [
                    self.copy(k * (X - 1) + d - 1, ref.at[pl.ds(0, h)], rx.at[which, k, d - 1], peer_x(d))
                    for d in range(1, X)
                ]
                for k in range(Z)
            ]
            self.p = [
                self.copy(Z * (X - 1) + i, ref.at[pl.ds(0, h), pl.ds(0, c), :], rp.at[which, i], peer_zy(d, e))
                for i, (d, e) in enumerate(plane)
            ]

        def copy(self, index, src, dst, peer):
            return pltpu.make_async_remote_copy(
                src_ref=src,
                dst_ref=dst,
                send_sem=rs_send.at[self.which, index],
                recv_sem=rs_recv.at[self.which, index],
                device_id={"shot": peer},
                device_id_type=MESH,
            )

        def start_x(self, k):
            for to in range(X):
                d = lax.rem(to - x + X, X)
                slot = lax.max(d - 1, 0)
                begin = h * (at_edge, in_middle)[k][to]
                copy = self.copy(
                    k * (X - 1) + slot, self.ref.at[pl.ds(begin, h)], rx.at[self.which, k, slot], peer_x(d)
                )
                pl.when(d > 0)(copy.start)

        def then_plane(self, k):
            for copy in self.x[k]:
                copy.wait_recv()
            begin = h * chosen(x, (at_edge, in_middle)[k])
            for r in range(h):
                total = self.ref[begin + r]
                for d in range(1, X):
                    total = total + rx[self.which, k, d - 1, r]
                sx[self.which, k * h + r] = total
            d = lax.rem(k - z + Z, Z)
            for e in range(Y):
                slot = d * Y + e - 1 if e > 0 else lax.max(d * Y - 1, 0)
                copy = self.copy(
                    Z * (X - 1) + slot,
                    sx.at[
                        self.which,
                        pl.ds(k * h, h),
                        pl.ds(pl.multiple_of(lax.rem(y + e, Y) * c, c), c),
                        :,
                    ],
                    rp.at[self.which, slot],
                    peer_zy(d, e),
                )
                if e > 0:
                    copy.start()
                else:
                    pl.when(d > 0)(copy.start)

        def piece(self):
            for copy in self.p:
                copy.wait_recv()
            total = sx[self.which, pl.ds(z * h, h), pl.ds(pl.multiple_of(y * c, c), c), :]
            for i in range(len(self.p)):
                total = total + rp[self.which, i]
            return total

        def leave(self):
            for copy in sum(self.x, []) + self.p:
                copy.wait_send()

    reduce_g, reduce_i = Reduce(0, G), Reduce(1, I)

    halo_u[1].arrive()
    over_edges(wave_row(1))
    halo_u[2].start()
    over(H, R - H, adjoint_row(1))
    receive(2)
    halo_w[1].arrive()
    over_edges(adjoint_row(1))
    halo_w[2].start()
    depth(U.at[2], zu)
    over(H, R - H, wave_row(2))
    halo_u[2].arrive()
    over_edges(wave_row(2))
    halo_u[3].start()
    depth(W.at[2], zw)
    over(H, R - H, adjoint_row(2))
    depth(U.at[3], zu)
    over(H, R - H, wave_row(3))
    reduce_g.start_x(1)

    def light(r):
        one, two, three = (U[(t, *centre(r))] for t in range(1, 4))
        I[r] = (one * one + two * two) + three * three

    over(0, R, light)
    reduce_i.start_x(1)
    reduce_i.start_x(0)
    receive(3)
    halo_w[2].arrive()
    over_edges(adjoint_row(2))
    halo_u[3].arrive()
    over_edges(wave_row(3))
    reduce_g.start_x(0)
    halo_u[4].start()
    reduce_g.then_plane(1)
    halo_w[3].start()
    reduce_i.then_plane(1)
    reduce_i.then_plane(0)
    depth(W.at[3], zw)
    over(H, R - H, adjoint_row(3, last=True))

    depth(U.at[STEPS + 1], zu)

    def before_update(r):
        L[r] = laplace(U.at[STEPS + 1], zu, r)
        U[(STEPS + 2, *centre(r))] = (
            2.0 * U[(STEPS + 1, *centre(r))] - U[(STEPS, *centre(r))]
        ) + injected(r, wavelet[0, STEPS])

    over(H, R - H, before_update)
    reduce_g.then_plane(0)
    illumination = reduce_i.piece()
    gradient = reduce_g.piece()

    E[pl.ds(H, h), pl.ds(c, c), :] = gradient / jnp.sqrt(illumination + 1.0)

    def index_of(d, e):
        return (d + reach) * 3 + e + 1

    def to_near(d, e):
        return pltpu.make_async_remote_copy(
            src_ref=E.at[pl.ds(H, h), pl.ds(c, c), :],
            dst_ref=E.at[pl.ds(H - d * h, h), pl.ds(c - e * c, c), :],
            send_sem=near_send.at[index_of(d, e)],
            recv_sem=near_recv.at[index_of(-d, -e)],
            device_id=owner(d, e),
            device_id_type=MESH,
        )

    for d, e in near:
        pl.when(is_near(d, e))(to_near(d, e).start)
    halo_u[STEPS + 1].arrive()
    over_edges(before_update)
    for d, e in near:
        pl.when(is_near(d, e))(to_near(-d, -e).wait_recv)

    row = h * pair_of(x, z)
    at_first = y * c - c + lax.broadcasted_iota(jnp.int32, (1, 3 * c, 1), 1)
    face_first = (at_first >= 0) & (at_first + 1 < NX)
    face_third = lax.broadcasted_iota(jnp.int32, (1, 1, LANES), 2) < LANES - 1

    def conduct(rise):
        return rise / (1.0 + rise * rise)

    smoothed = E[...]
    for turn in range(PASSES):
        rows = smoothed.shape[0]
        at_second = (start_second + row - H + turn + 1) + lax.broadcasted_iota(
            jnp.int32, (rows - 1, 1, 1), 0
        )
        face_second = (at_second > 0) & (at_second < NY)
        second = jnp.where(face_second, conduct(smoothed[1:] - smoothed[:-1]), 0.0)
        field = smoothed[1:-1]
        along_first = jnp.where(face_first, conduct(pltpu.roll(field, 3 * c - 1, 1) - field), 0.0)
        along_third = jnp.where(face_third, conduct(pltpu.roll(field, LANES - 1, 2) - field), 0.0)
        change = (
            (along_first - pltpu.roll(along_first, 1, 1))
            + (second[1:] - second[:-1])
            + (along_third - pltpu.roll(along_third, 1, 2))
        )
        smoothed = field + diffuse_rate * change
    mine = pl.ds(row, h), pl.ds(pl.multiple_of(y * c, c), c), slice(None)
    S[mine] = jnp.clip(speed[mine] - step_length * smoothed[:, c : 2 * c], speed_floor, speed_ceiling)

    def share(index, part, peer):
        return pltpu.make_async_remote_copy(
            src_ref=part,
            dst_ref=part,
            send_sem=ag_send.at[index],
            recv_sem=ag_recv.at[index],
            device_id={"shot": peer},
            device_id_type=MESH,
        )

    first_slot = Z * (X - 1)
    by_plane = [
        share(first_slot + i, S.at[mine], peer_zy(d, e)) for i, (d, e) in enumerate(plane)
    ]
    for copy in by_plane:
        copy.start()
    halo_w[3].arrive()
    over_edges(adjoint_row(3, last=True))
    by_x = []
    for k in range(Z):
        d = lax.rem(z - k + Z, Z)
        for e in range(Y):
            slot = first_slot + (d * Y + e - 1 if e > 0 else lax.max(d * Y - 1, 0))
            if e > 0:
                share(slot, S.at[mine], peer_zy(d, e)).wait_recv()
            else:
                pl.when(d > 0)(share(slot, S.at[mine], peer_zy(d, e)).wait_recv)
        part = S.at[pl.ds(h * chosen(x, (at_edge, in_middle)[k]), h)]
        by_x.append([share(k * (X - 1) + d - 1, part, peer_x(d)) for d in range(1, X)])
        for copy in by_x[k]:
            copy.start()

    def final_one(r):
        new_speed = S[r]
        speed_out[pl.ds(r, NX, stride=R), :] = new_speed
        new_square = new_speed * new_speed
        square[r] = new_square
        U[(STEPS + 2, *centre(r))] = U[(STEPS + 2, *centre(r))] + new_square * L[r]

    def final_two(r):
        wave_out[pl.ds(r, NX, stride=R), :] = (
            2.0 * U[(STEPS + 2, *centre(r))] - U[(STEPS + 1, *centre(r))]
        ) + (square[r] * laplace(U.at[STEPS + 2], zu, r) + injected(r, wavelet[0, STEPS + 1]))

    for copy in by_x[0]:
        copy.wait_recv()
    over_edges(final_one)
    halo_u[STEPS + 2].start()
    for copy in by_x[1]:
        copy.wait_recv()
    over(H, R - H, final_one)
    depth(U.at[STEPS + 2], zu)
    over(H, R - H, final_two)
    halo_u[STEPS + 2].arrive()
    over_edges(final_two)

    for halo in (*list(halo_u.values())[1:], *halo_w.values()):
        halo.leave()
    reduce_g.leave()
    reduce_i.leave()
    for d, e in near:
        pl.when(is_near(d, e))(to_near(d, e).wait_send)
    for copy in by_plane + sum(by_x, []):
        copy.wait_send()


def hand_over(wave, adjoint, speed, wave_out, adjoint_out, speed_out, sem):
    copies = [
        pltpu.make_async_copy(src, dst, sem.at[i])
        for i, (src, dst) in enumerate(((wave, wave_out), (adjoint, adjoint_out), (speed, speed_out)))
    ]
    for copy in copies:
        copy.start()
    for copy in copies:
        copy.wait()


def local(
    parts,
    boxes,
    wave_prev,
    wave_now,
    adjoint_prev,
    adjoint_now,
    velocity,
    source_cell,
    wavelet,
    receiver_cell,
    residual,
):
    X, Z, Y = parts
    NX, R, D = velocity.shape
    q, h, c = R // X, R // (X * Z), NX // Y
    f32 = jnp.float32
    flat = (NX * R, D)
    padded = (R + 2 * H, NX + 2 * PAD, D)
    plain = (R, NX, D)
    n_rs = Z * (X - 1) + Z * Y - 1
    n_near = 3 * (2 * -(-H // h) + 1)
    vmem, smem, anywhere = (
        pl.BlockSpec(memory_space=pltpu.VMEM),
        pl.BlockSpec(memory_space=pltpu.SMEM),
        pl.BlockSpec(memory_space=pl.ANY),
    )
    out = jax.ShapeDtypeStruct(flat, f32)
    kept = pltpu.VMEM(flat, f32)
    wave_out, adjoint_out, speed_out = pl.pallas_call(
        functools.partial(kernel, (X, Z, Y, boxes, NX, R)),
        out_shape=(kept, kept, kept),
        in_specs=[smem, smem, vmem, vmem] + [anywhere] * 5,
        out_specs=(vmem, vmem, vmem),
        scratch_shapes=[
            pltpu.VMEM((5, *flat), f32),
            pltpu.VMEM((6, *padded), f32),
            pltpu.VMEM((4, *padded), f32),
            pltpu.VMEM(plain, f32),
            pltpu.VMEM(plain, f32),
            pltpu.VMEM((STEPS, *plain), f32),
            pltpu.VMEM(plain, f32),
            pltpu.VMEM(plain, f32),
            pltpu.VMEM((2, Z, X - 1, h, NX, D), f32),
            pltpu.VMEM((2, Z * Y - 1, h, c, D), f32),
            pltpu.VMEM((2, q, NX, D), f32),
            pltpu.VMEM((h + 2 * H, 3 * c, D), f32),
            pltpu.VMEM(plain, f32),
            pltpu.VMEM(plain, f32),
            pltpu.VMEM(plain, f32),
            pltpu.VMEM(plain, f32),
            pltpu.SemaphoreType.DMA((5,)),
            pltpu.SemaphoreType.DMA((8, 2)),
            pltpu.SemaphoreType.DMA((8, 2)),
            pltpu.SemaphoreType.DMA((2, n_rs)),
            pltpu.SemaphoreType.DMA((2, n_rs)),
            pltpu.SemaphoreType.DMA((n_rs,)),
            pltpu.SemaphoreType.DMA((n_rs,)),
            pltpu.SemaphoreType.DMA((n_near,)),
            pltpu.SemaphoreType.DMA((n_near,)),
        ],
        compiler_params=pltpu.CompilerParams(
            collective_id=0, has_side_effects=True, vmem_limit_bytes=56 * 1024 * 1024
        ),
    )(
        source_cell,
        wavelet,
        receiver_cell,
        residual.transpose(1, 0, 2),
        wave_prev.reshape(flat),
        wave_now.reshape(flat),
        adjoint_prev.reshape(flat),
        adjoint_now.reshape(flat),
        velocity.reshape(flat),
    )
    wave_out, adjoint_out, speed_out = pl.pallas_call(
        hand_over,
        out_shape=(out, out, out),
        in_specs=[vmem] * 3,
        out_specs=(anywhere,) * 3,
        scratch_shapes=[pltpu.SemaphoreType.DMA((3,))],
    )(*(pltpu.with_memory_space_constraint(a, pltpu.VMEM) for a in (wave_out, adjoint_out, speed_out)))
    field = (1, NX, R, D)
    return wave_out.reshape(field), adjoint_out.reshape(field), speed_out.reshape(field[1:])


def solution(mesh):
    shots, boxes = mesh.shape["shot"], mesh.shape["box"]
    parts = {64: (4, 2, 8), 16: (4, 2, 2), 8: (4, 2, 1)}[shots]
    return jax.shard_map(
        functools.partial(local, parts, boxes),
        mesh=mesh,
        in_specs=(
            P("shot", None, "box", None),
            P("shot", None, "box", None),
            P("shot", None, "box", None),
            P("shot", None, "box", None),
            P(None, "box", None),
            P("shot"),
            P("shot", None),
            P("shot", None),
            P("shot", None, None),
        ),
        out_specs=(
            P("shot", None, "box", None),
            P("shot", None, "box", None),
            P(None, "box", None),
        ),
        check_vma=False,
    )
```

```python
import functools

import jax
import jax.numpy as jnp
from jax import lax
from jax.experimental import pallas as pl
from jax.experimental.pallas import tpu as pltpu
from jax.sharding import PartitionSpec as P

MESH = pl.DeviceIdType.MESH
STEPS = 3
FINAL = 2
PASSES = 4
RDEPTH = 2
LANES = 128
H = 4
PAD = 8

stencil_weights = (-205.0 / 72.0, 8.0 / 5.0, -1.0 / 5.0, 8.0 / 315.0, -1.0 / 560.0)
diffuse_rate = 0.1
step_length = 0.1
speed_floor = 0.16
speed_ceiling = 0.44


def kernel(
    sizes,
    source_cell,
    wavelet,
    receiver_cell,
    residual,
    wave_prev,
    wave_now,
    adjoint_prev,
    adjoint_now,
    velocity,
    wave_out,
    adjoint_out,
    speed_out,
    staged,
    U,
    W,
    speed,
    square,
    received,
    G,
    I,
    rx,
    rp,
    sx,
    E,
    S,
    L,
    zu,
    zw,
    in_sem,
    halo_send,
    halo_recv,
    rs_send,
    rs_recv,
    ag_send,
    ag_recv,
    near_send,
    near_recv,
):
    X, Z, Y, boxes, NX, R = sizes
    NY = R * boxes
    h, c = R // (X * Z), NX // Y
    shot, box = lax.axis_index("shot"), lax.axis_index("box")
    x = lax.div(shot, Z * Y)
    z = lax.rem(lax.div(shot, Y), Z)
    y = lax.rem(shot, Y)
    lower, upper = lax.max(box - 1, 0), lax.min(box + 1, boxes - 1)
    has_lower, has_upper = box > 0, box < boxes - 1

    def peer_x(d):
        return (lax.rem(x + d, X) * Z + z) * Y + y

    def peer_zy(d, e):
        return (x * Z + lax.rem(z + d, Z)) * Y + lax.rem(y + e, Y)

    at_edge = (1, 7, 0, 6)
    in_middle = (2, 3, 4, 5)

    def chosen(index, table):
        value = table[0]
        for i in range(1, len(table)):
            value = jnp.where(index == i, table[i], value)
        return value

    def pair_of(x, z):
        return jnp.where(z == 0, chosen(x, at_edge), chosen(x, in_middle))

    plane = [(d, e) for d in range(Z) for e in range(Y) if (d, e) != (0, 0)]

    pieces = X * Z
    place = box * pieces + pair_of(x, z)
    reach = -(-H // h)
    beside = [e for e in (-1, 0, 1) if Y > 1 or e == 0]
    near = [(d, e) for d in range(-reach, reach + 1) for e in beside if (d, e) != (0, 0)]

    def is_near(d, e):
        return (place + d >= 0) & (place + d < boxes * pieces) & (y + e >= 0) & (y + e < Y)

    def owner(d, e):
        other = lax.clamp(0, place + d, boxes * pieces - 1)
        pair = lax.rem(other, pieces)
        to_x = chosen(pair, tuple((at_edge + in_middle).index(p) % X for p in range(pieces)))
        to_z = chosen(pair, tuple((at_edge + in_middle).index(p) // X for p in range(pieces)))
        return {
            "shot": (to_x * Z + to_z) * Y + lax.clamp(0, y + e, Y - 1),
            "box": lax.div(other, pieces),
        }

    E[...] = jnp.zeros_like(E)

    loads = [
        pltpu.make_async_copy(ref, staged.at[i], in_sem.at[i])
        for i, ref in enumerate((wave_now, adjoint_now, wave_prev, adjoint_prev, velocity))
    ]
    for load in loads:
        load.start()

    barrier = pltpu.get_barrier_semaphore()
    peers = [peer_x(d) for d in range(1, X)] + [peer_zy(d, e) for d, e in plane]
    for peer in peers:
        pl.semaphore_signal(barrier, inc=1, device_id={"shot": peer}, device_id_type=MESH)

    @pl.when(has_lower)
    def _():
        pl.semaphore_signal(barrier, inc=1, device_id={"box": lower}, device_id_type=MESH)

    @pl.when(has_upper)
    def _():
        pl.semaphore_signal(barrier, inc=1, device_id={"box": upper}, device_id_type=MESH)

    count = len(peers) + has_lower.astype(jnp.int32) + has_upper.astype(jnp.int32)
    for d, e in near:

        @pl.when(is_near(d, e))
        def _(d=d, e=e):
            pl.semaphore_signal(barrier, inc=1, device_id=owner(d, e), device_id_type=MESH)

        count = count + is_near(d, e).astype(jnp.int32)

    pad = jnp.zeros((R, PAD, LANES), jnp.float32)
    edge = jnp.zeros((H, NX, LANES), jnp.float32)
    for fields, slots in ((U, range(1, 6)), (W, range(1, 4))):
        for slot in slots:
            fields[slot, H : H + R, :PAD, :] = pad
            fields[slot, H : H + R, PAD + NX :, :] = pad

    @pl.when(box == 0)
    def _():
        for fields, slots in ((U, range(1, 6)), (W, range(1, 4))):
            for slot in slots:
                fields[slot, :H, PAD : PAD + NX, :] = edge

    @pl.when(box == boxes - 1)
    def _():
        for fields, slots in ((U, range(1, 6)), (W, range(1, 4))):
            for slot in slots:
                fields[slot, H + R :, PAD : PAD + NX, :] = edge

    class Halo:
        def __init__(self, ref, index):
            def rows(start):
                return ref.at[pl.ds(start, H), pl.ds(PAD, NX), :]

            self.down = pltpu.make_async_remote_copy(
                src_ref=rows(H),
                dst_ref=rows(H + R),
                send_sem=halo_send.at[index, 0],
                recv_sem=halo_recv.at[index, 0],
                device_id={"box": lower},
                device_id_type=MESH,
            )
            self.up = pltpu.make_async_remote_copy(
                src_ref=rows(R),
                dst_ref=rows(0),
                send_sem=halo_send.at[index, 1],
                recv_sem=halo_recv.at[index, 1],
                device_id={"box": upper},
                device_id_type=MESH,
            )

        def start(self):
            pl.when(has_lower)(self.down.start)
            pl.when(has_upper)(self.up.start)

        def arrive(self):
            pl.when(has_lower)(self.up.wait_recv)
            pl.when(has_upper)(self.down.wait_recv)

        def leave(self):
            pl.when(has_lower)(self.down.wait_send)
            pl.when(has_upper)(self.up.wait_send)

    halo_u = {t: Halo(U.at[t], t - 1) for t in range(1, 6)}
    halo_w = {t: Halo(W.at[t], 4 + t) for t in range(1, 4)}

    lane = lax.broadcasted_iota(jnp.int32, (1, LANES), 1)
    first = lax.broadcasted_iota(jnp.int32, (NX, 1), 0)
    flat = lax.broadcasted_iota(jnp.int32, (NX, LANES), 0) * (NY * LANES) + lax.broadcasted_iota(
        jnp.int32, (NX, LANES), 1
    )
    start_second = box * R
    source = source_cell[0]

    def over(begin, end, body):
        lax.fori_loop(begin, end, lambda r, carry: (body(r), carry)[1], 0)

    def over_edges(body):
        def step(i, carry):
            body(jnp.where(i < H, i, i + (R - 2 * H)))
            return carry

        lax.fori_loop(0, 2 * H, step, 0)

    def turned(i, r):
        return staged[i, pl.ds(r, NX, stride=R), :]

    def centre(r):
        return (H + r, pl.ds(PAD, NX), slice(None))

    apart = lax.broadcasted_iota(jnp.int32, (LANES, LANES), 0) - lax.broadcasted_iota(
        jnp.int32, (LANES, LANES), 1
    )
    along_depth = jnp.where(apart == 0, 3.0 * stencil_weights[0], 0.0)
    for k in range(1, 5):
        along_depth = along_depth + jnp.where((apart == k) | (apart == -k), stencil_weights[k], 0.0)

    def depth(ref, out):
        field = ref[pl.ds(H, R), pl.ds(PAD, NX), :].reshape(R * NX, LANES)
        out[...] = lax.dot_general(
            field,
            along_depth,
            (((1,), (0,)), ((), ())),
            precision=lax.Precision.HIGHEST,
            preferred_element_type=jnp.float32,
        ).reshape(R, NX, LANES)

    def laplace(ref, along, r):
        summed = along[r]
        for k in range(1, 5):
            around = (ref[H + r + k, pl.ds(PAD, NX), :] + ref[H + r - k, pl.ds(PAD, NX), :]) + (
                ref[H + r, pl.ds(PAD + k, NX), :] + ref[H + r, pl.ds(PAD - k, NX), :]
            )
            summed = summed + stencil_weights[k] * around
        return summed

    def injected(r, amplitude):
        return jnp.where(flat == source - (start_second + r) * LANES, amplitude, 0.0)

    def wave_row(t):
        now, early, later = U.at[t], U.at[t - 1], U.at[t + 1]
        amplitude = wavelet[0, t - 1]

        def body(r):
            field = now[centre(r)]
            second_diff = square[r] * laplace(now, zu, r) + injected(r, amplitude)
            later[centre(r)] = (2.0 * field - early[centre(r)]) + second_diff
            term = W[(t, *centre(r))] * second_diff
            G[r] = term if t == 1 else G[r] + term

        return body

    def adjoint_row(t, last=False):
        now, early = W.at[t], W.at[t - 1]

        def body(r):
            value = (2.0 * now[centre(r)] - early[centre(r)]) + (
                square[r] * laplace(now, zw, r) + received[t - 1, r]
            )
            if last:
                adjoint_out[pl.ds(r, NX, stride=R), :] = value
            else:
                W[(t + 1, *centre(r))] = value

        return body

    loads[0].wait()

    def turn_wave(r):
        U[(1, *centre(r))] = turned(0, r)

    over(0, R, turn_wave)
    pl.semaphore_wait(barrier, count)
    halo_u[1].start()
    loads[1].wait()

    def turn_adjoint(r):
        W[(1, *centre(r))] = turned(1, r)

    over(0, R, turn_adjoint)
    depth(U.at[1], zu)
    loads[2].wait()
    loads[3].wait()
    loads[4].wait()

    def turn_rest(r):
        U[(0, *centre(r))] = turned(2, r)
        W[(0, *centre(r))] = turned(3, r)
        v = turned(4, r)
        speed[r] = v
        square[r] = v * v

    over(0, R, turn_rest)
    over(H, R - H, wave_row(1))

    def receive(t):
        shape = (R, NX, LANES)
        here = (
            lax.broadcasted_iota(jnp.int32, shape, 1) * NY
            + lax.broadcasted_iota(jnp.int32, shape, 0)
            + start_second
        ) * LANES + RDEPTH
        picks = jnp.where(here == receiver_cell[...].reshape(1, 1, LANES), 1.0, 0.0)
        picks = picks.astype(jnp.bfloat16).reshape(R * NX, LANES)
        at_depth = lax.broadcasted_iota(jnp.int32, (LANES, LANES), 0) == RDEPTH
        rest, total = jnp.where(at_depth, residual[t - 1], 0.0), None
        for _ in range(3):
            part = rest.astype(jnp.bfloat16)
            rest = rest - part.astype(jnp.float32)
            picked = lax.dot_general(
                picks, part, (((1,), (1,)), ((), ())), preferred_element_type=jnp.float32
            )
            total = picked if total is None else total + picked
        received[t - 1] = total.reshape(shape)

    receive(1)
    halo_u[1].leave()
    halo_w[1].start()
    depth(W.at[1], zw)


    class Reduce:
        def __init__(self, which, ref):
            self.ref, self.which = ref, which
            self.x = [
                [
                    self.copy(k * (X - 1) + d - 1, ref.at[pl.ds(0, h)], rx.at[which, k, d - 1], peer_x(d))
                    for d in range(1, X)
                ]
                for k in range(Z)
            ]
            self.p = [
                self.copy(Z * (X - 1) + i, ref.at[pl.ds(0, h), pl.ds(0, c), :], rp.at[which, i], peer_zy(d, e))
                for i, (d, e) in enumerate(plane)
            ]

        def copy(self, index, src, dst, peer):
            return pltpu.make_async_remote_copy(
                src_ref=src,
                dst_ref=dst,
                send_sem=rs_send.at[self.which, index],
                recv_sem=rs_recv.at[self.which, index],
                device_id={"shot": peer},
                device_id_type=MESH,
            )

        def start_x(self, k):
            for to in range(X):
                d = lax.rem(to - x + X, X)
                slot = lax.max(d - 1, 0)
                begin = h * (at_edge, in_middle)[k][to]
                copy = self.copy(
                    k * (X - 1) + slot, self.ref.at[pl.ds(begin, h)], rx.at[self.which, k, slot], peer_x(d)
                )
                pl.when(d > 0)(copy.start)

        def then_plane(self, k):
            for copy in self.x[k]:
                copy.wait_recv()
            begin = h * chosen(x, (at_edge, in_middle)[k])
            for r in range(h):
                total = self.ref[begin + r]
                for d in range(1, X):
                    total = total + rx[self.which, k, d - 1, r]
                sx[self.which, k * h + r] = total
            d = lax.rem(k - z + Z, Z)
            for e in range(Y):
                slot = d * Y + e - 1 if e > 0 else lax.max(d * Y - 1, 0)
                copy = self.copy(
                    Z * (X - 1) + slot,
                    sx.at[
                        self.which,
                        pl.ds(k * h, h),
                        pl.ds(pl.multiple_of(lax.rem(y + e, Y) * c, c), c),
                        :,
                    ],
                    rp.at[self.which, slot],
                    peer_zy(d, e),
                )
                if e > 0:
                    copy.start()
                else:
                    pl.when(d > 0)(copy.start)

        def piece(self):
            for copy in self.p:
                copy.wait_recv()
            total = sx[self.which, pl.ds(z * h, h), pl.ds(pl.multiple_of(y * c, c), c), :]
            for i in range(len(self.p)):
                total = total + rp[self.which, i]
            return total

        def leave(self):
            for copy in sum(self.x, []) + self.p:
                copy.wait_send()

    reduce_g, reduce_i = Reduce(0, G), Reduce(1, I)

    halo_u[1].arrive()
    over_edges(wave_row(1))
    halo_u[2].start()
    over(H, R - H, adjoint_row(1))
    receive(2)
    halo_w[1].arrive()
    over_edges(adjoint_row(1))
    halo_w[2].start()
    depth(U.at[2], zu)
    over(H, R - H, wave_row(2))
    halo_u[2].arrive()
    over_edges(wave_row(2))
    halo_u[3].start()

    def light(r):
        one, two, three = (U[(t, *centre(r))] for t in range(1, 4))
        I[r] = (one * one + two * two) + three * three

    over(0, R, light)
    reduce_i.start_x(1)
    reduce_i.start_x(0)
    depth(W.at[2], zw)
    over(H, R - H, adjoint_row(2))
    depth(U.at[3], zu)
    over(H, R - H, wave_row(3))
    reduce_g.start_x(1)
    receive(3)
    halo_w[2].arrive()
    over_edges(adjoint_row(2))
    halo_u[3].arrive()
    over_edges(wave_row(3))
    reduce_g.start_x(0)
    halo_u[4].start()
    reduce_g.then_plane(1)
    halo_w[3].start()
    reduce_i.then_plane(1)
    reduce_i.then_plane(0)
    depth(W.at[3], zw)
    over(H, R - H, adjoint_row(3, last=True))

    depth(U.at[STEPS + 1], zu)

    def before_update(r):
        L[r] = laplace(U.at[STEPS + 1], zu, r)
        U[(STEPS + 2, *centre(r))] = (
            2.0 * U[(STEPS + 1, *centre(r))] - U[(STEPS, *centre(r))]
        ) + injected(r, wavelet[0, STEPS])

    over(H, R - H, before_update)
    reduce_g.then_plane(0)
    illumination = reduce_i.piece()
    gradient = reduce_g.piece()

    E[pl.ds(H, h), pl.ds(c, c), :] = gradient / jnp.sqrt(illumination + 1.0)

    def index_of(d, e):
        return (d + reach) * 3 + e + 1

    def to_near(d, e):
        return pltpu.make_async_remote_copy(
            src_ref=E.at[pl.ds(H, h), pl.ds(c, c), :],
            dst_ref=E.at[pl.ds(H - d * h, h), pl.ds(c - e * c, c), :],
            send_sem=near_send.at[index_of(d, e)],
            recv_sem=near_recv.at[index_of(-d, -e)],
            device_id=owner(d, e),
            device_id_type=MESH,
        )

    for d, e in near:
        pl.when(is_near(d, e))(to_near(d, e).start)
    halo_u[STEPS + 1].arrive()
    over_edges(before_update)
    for d, e in near:
        pl.when(is_near(d, e))(to_near(-d, -e).wait_recv)

    row = h * pair_of(x, z)
    at_first = y * c - c + lax.broadcasted_iota(jnp.int32, (1, 3 * c, 1), 1)
    face_first = (at_first >= 0) & (at_first + 1 < NX)
    face_third = lax.broadcasted_iota(jnp.int32, (1, 1, LANES), 2) < LANES - 1

    def conduct(rise):
        return rise / (1.0 + rise * rise)

    smoothed = E[...]
    for turn in range(PASSES):
        rows = smoothed.shape[0]
        at_second = (start_second + row - H + turn + 1) + lax.broadcasted_iota(
            jnp.int32, (rows - 1, 1, 1), 0
        )
        face_second = (at_second > 0) & (at_second < NY)
        second = jnp.where(face_second, conduct(smoothed[1:] - smoothed[:-1]), 0.0)
        field = smoothed[1:-1]
        along_first = jnp.where(face_first, conduct(pltpu.roll(field, 3 * c - 1, 1) - field), 0.0)
        along_third = jnp.where(face_third, conduct(pltpu.roll(field, LANES - 1, 2) - field), 0.0)
        change = (
            (along_first - pltpu.roll(along_first, 1, 1))
            + (second[1:] - second[:-1])
            + (along_third - pltpu.roll(along_third, 1, 2))
        )
        smoothed = field + diffuse_rate * change
    mine = pl.ds(row, h), pl.ds(pl.multiple_of(y * c, c), c), slice(None)
    S[mine] = jnp.clip(speed[mine] - step_length * smoothed[:, c : 2 * c], speed_floor, speed_ceiling)

    def share(index, part, peer):
        return pltpu.make_async_remote_copy(
            src_ref=part,
            dst_ref=part,
            send_sem=ag_send.at[index],
            recv_sem=ag_recv.at[index],
            device_id={"shot": peer},
            device_id_type=MESH,
        )

    first_slot = Z * (X - 1)
    by_plane = [
        share(first_slot + i, S.at[mine], peer_zy(d, e)) for i, (d, e) in enumerate(plane)
    ]
    for copy in by_plane:
        copy.start()
    halo_w[3].arrive()
    over_edges(adjoint_row(3, last=True))
    by_x = []
    for k in range(Z):
        d = lax.rem(z - k + Z, Z)
        for e in range(Y):
            slot = first_slot + (d * Y + e - 1 if e > 0 else lax.max(d * Y - 1, 0))
            if e > 0:
                share(slot, S.at[mine], peer_zy(d, e)).wait_recv()
            else:
                pl.when(d > 0)(share(slot, S.at[mine], peer_zy(d, e)).wait_recv)
        part = S.at[pl.ds(h * chosen(x, (at_edge, in_middle)[k]), h)]
        by_x.append([share(k * (X - 1) + d - 1, part, peer_x(d)) for d in range(1, X)])
        for copy in by_x[k]:
            copy.start()

    def final_one(r):
        new_speed = S[r]
        speed_out[pl.ds(r, NX, stride=R), :] = new_speed
        new_square = new_speed * new_speed
        square[r] = new_square
        U[(STEPS + 2, *centre(r))] = U[(STEPS + 2, *centre(r))] + new_square * L[r]

    def final_two(r):
        wave_out[pl.ds(r, NX, stride=R), :] = (
            2.0 * U[(STEPS + 2, *centre(r))] - U[(STEPS + 1, *centre(r))]
        ) + (square[r] * laplace(U.at[STEPS + 2], zu, r) + injected(r, wavelet[0, STEPS + 1]))

    for copy in by_x[0]:
        copy.wait_recv()
    over_edges(final_one)
    halo_u[STEPS + 2].start()
    for copy in by_x[1]:
        copy.wait_recv()
    over(H, R - H, final_one)
    depth(U.at[STEPS + 2], zu)
    over(H, R - H, final_two)
    halo_u[STEPS + 2].arrive()
    over_edges(final_two)

    for halo in (*list(halo_u.values())[1:], *halo_w.values()):
        halo.leave()
    reduce_g.leave()
    reduce_i.leave()
    for d, e in near:
        pl.when(is_near(d, e))(to_near(d, e).wait_send)
    for copy in by_plane + sum(by_x, []):
        copy.wait_send()


def hand_over(wave, adjoint, speed, wave_out, adjoint_out, speed_out, sem):
    copies = [
        pltpu.make_async_copy(src, dst, sem.at[i])
        for i, (src, dst) in enumerate(((wave, wave_out), (adjoint, adjoint_out), (speed, speed_out)))
    ]
    for copy in copies:
        copy.start()
    for copy in copies:
        copy.wait()


def local(
    parts,
    boxes,
    wave_prev,
    wave_now,
    adjoint_prev,
    adjoint_now,
    velocity,
    source_cell,
    wavelet,
    receiver_cell,
    residual,
):
    X, Z, Y = parts
    NX, R, D = velocity.shape
    q, h, c = R // X, R // (X * Z), NX // Y
    f32 = jnp.float32
    flat = (NX * R, D)
    padded = (R + 2 * H, NX + 2 * PAD, D)
    plain = (R, NX, D)
    n_rs = Z * (X - 1) + Z * Y - 1
    n_near = 3 * (2 * -(-H // h) + 1)
    vmem, smem, anywhere = (
        pl.BlockSpec(memory_space=pltpu.VMEM),
        pl.BlockSpec(memory_space=pltpu.SMEM),
        pl.BlockSpec(memory_space=pl.ANY),
    )
    out = jax.ShapeDtypeStruct(flat, f32)
    kept = pltpu.VMEM(flat, f32)
    wave_out, adjoint_out, speed_out = pl.pallas_call(
        functools.partial(kernel, (X, Z, Y, boxes, NX, R)),
        out_shape=(kept, kept, kept),
        in_specs=[smem, smem, vmem, vmem] + [anywhere] * 5,
        out_specs=(vmem, vmem, vmem),
        scratch_shapes=[
            pltpu.VMEM((5, *flat), f32),
            pltpu.VMEM((6, *padded), f32),
            pltpu.VMEM((4, *padded), f32),
            pltpu.VMEM(plain, f32),
            pltpu.VMEM(plain, f32),
            pltpu.VMEM((STEPS, *plain), f32),
            pltpu.VMEM(plain, f32),
            pltpu.VMEM(plain, f32),
            pltpu.VMEM((2, Z, X - 1, h, NX, D), f32),
            pltpu.VMEM((2, Z * Y - 1, h, c, D), f32),
            pltpu.VMEM((2, q, NX, D), f32),
            pltpu.VMEM((h + 2 * H, 3 * c, D), f32),
            pltpu.VMEM(plain, f32),
            pltpu.VMEM(plain, f32),
            pltpu.VMEM(plain, f32),
            pltpu.VMEM(plain, f32),
            pltpu.SemaphoreType.DMA((5,)),
            pltpu.SemaphoreType.DMA((8, 2)),
            pltpu.SemaphoreType.DMA((8, 2)),
            pltpu.SemaphoreType.DMA((2, n_rs)),
            pltpu.SemaphoreType.DMA((2, n_rs)),
            pltpu.SemaphoreType.DMA((n_rs,)),
            pltpu.SemaphoreType.DMA((n_rs,)),
            pltpu.SemaphoreType.DMA((n_near,)),
            pltpu.SemaphoreType.DMA((n_near,)),
        ],
        compiler_params=pltpu.CompilerParams(
            collective_id=0, has_side_effects=True, vmem_limit_bytes=56 * 1024 * 1024
        ),
    )(
        source_cell,
        wavelet,
        receiver_cell,
        residual.transpose(1, 0, 2),
        wave_prev.reshape(flat),
        wave_now.reshape(flat),
        adjoint_prev.reshape(flat),
        adjoint_now.reshape(flat),
        velocity.reshape(flat),
    )
    wave_out, adjoint_out, speed_out = pl.pallas_call(
        hand_over,
        out_shape=(out, out, out),
        in_specs=[vmem] * 3,
        out_specs=(anywhere,) * 3,
        scratch_shapes=[pltpu.SemaphoreType.DMA((3,))],
    )(*(pltpu.with_memory_space_constraint(a, pltpu.VMEM) for a in (wave_out, adjoint_out, speed_out)))
    field = (1, NX, R, D)
    return wave_out.reshape(field), adjoint_out.reshape(field), speed_out.reshape(field[1:])


def solution(mesh):
    shots, boxes = mesh.shape["shot"], mesh.shape["box"]
    parts = {64: (4, 2, 8), 16: (4, 2, 2), 8: (4, 2, 1)}[shots]
    return jax.shard_map(
        functools.partial(local, parts, boxes),
        mesh=mesh,
        in_specs=(
            P("shot", None, "box", None),
            P("shot", None, "box", None),
            P("shot", None, "box", None),
            P("shot", None, "box", None),
            P(None, "box", None),
            P("shot"),
            P("shot", None),
            P("shot", None),
            P("shot", None, None),
        ),
        out_specs=(
            P("shot", None, "box", None),
            P("shot", None, "box", None),
            P(None, "box", None),
        ),
        check_vma=False,
    )
```
